256 devices in a mesh: gx: 16 (over z_hi, x), gy: 16 (over z_lo, y, core).
Axes of the slice: x: 4, y: 4, z: 8 (z_hi: 4, z_lo: 2; z = z_hi * 2 + z_lo), core: 2. Of those that a mesh axis runs over, the one named last changes fastest.
Arguments:
- fields: float32 [6, 48, 128, 2048], P(None, None, 'gx', 'gy'), may hold values from -6 to 6
- adjoint: float32 [6, 48, 128, 2048], P(None, None, 'gx', 'gy'), may hold values from -6 to 6
- permittivity: float32 [48, 128, 2048], P(None, 'gx', 'gy'), may hold values from 1 to 12
- lists: int32 [256, 128], replicated, may hold values from 0 to 255, all different within a row
- mask: int32 [256], replicated, may hold values 0 or 1
Outputs:
- fields_next: float32 [6, 48, 128, 2048], P(None, None, 'gx', 'gy')
- adjoint_next: float32 [6, 48, 128, 2048], P(None, None, 'gx', 'gy')
- sensitivity: float32 [48, 128, 2048], P(None, 'gx', 'gy')
- farfield: float32 [256, 8, 256], P(('gx', 'gy'))
The draws below stay inside these ranges and needn't reach their ends.
Inputs may be any that keep to these rules, and one draw needn't show every extreme that they name: `lists`: each row names 128 different direction blocks, and every block is named by some row.
All inputs are finite; a program needn't handle non-finite values.
Results may differ from the reference program's by a relative error of at most 0.0003.
Values sent between devices are 32-bit elements; how exact they have to be, the bound alone decides.
A program may use at most 64 MiB of HBM per device.

```python
import math
import jax
import jax.numpy as jnp
from jax import lax

CX = 8
CY = 128
NZ = 48
DIRS_U = 256
DIRS_V = 256
NX = 128
NY = 2048
TILES = 256
LIST = 128
URB = 1
ZM = 36
N_GY = 16


def set_ends(result, own_key, low, high):
    extent = result.shape
    spot = [jax.random.randint(jax.random.fold_in(own_key, axis), (), 0, extent[axis]) for axis in range(len(extent))]
    result = result.at[tuple(spot)].set(low)
    longest = extent.index(max(extent))
    spot[longest] = (spot[longest] + 1) % extent[longest]
    return result.at[tuple(spot)].set(high)


def levels(own_key, shape, pieces, low, high):
    loudness = 1.0
    for position, blocks in pieces:
        draws = jax.random.uniform(jax.random.fold_in(jax.random.fold_in(own_key, 6), position), (blocks,), jnp.float32, low / len(pieces), high / len(pieces))
        loudness = loudness * jnp.repeat(jnp.exp(draws), shape[position] // blocks).reshape((-1,) + (1,) * (len(shape) - 1 - position))
    return loudness


def choose_distinct(stream_key, rows, count, top, lift):
    order = jax.random.permutation(jax.random.fold_in(stream_key, 1), count)
    favour = order
    for power in range(3):
        favour = favour * favour // count
    favour = favour * lift // count
    chance = jax.random.randint(jax.random.fold_in(stream_key, 2), (rows, count), 0, 4096) + favour
    sure = jax.random.permutation(jax.random.fold_in(stream_key, 3), rows)[jnp.arange(count) % rows]
    chance = jnp.where(jnp.arange(rows)[:, None] == sure[None, :], 1 << 14, chance)
    priority = chance * count + jnp.arange(count)
    return lax.top_k(priority.astype(jnp.int32), top)[1].astype(jnp.int32)


def noise(own_key, extent, width, reach, pieces=(), held_as=jnp.bfloat16):
    level = levels(own_key, extent, pieces, -0.22, 0.18) if pieces else 1.0
    result = jax.random.normal(own_key, extent, jnp.float32) * width * level
    return jnp.minimum(jnp.maximum(result, -reach), reach).astype(held_as)


def setup_inputs(seed: int = 0) -> dict:
    streams_of = jax.random.split(jax.random.key(seed), 6)
    fields = noise(streams_of[0], (6, NZ, NX, NY), 1.0, 6.0, ((2, 16), (3, 16)), jnp.float32)
    adjoint = noise(streams_of[1], (6, NZ, NX, NY), 1.0, 6.0, ((2, 16), (3, 16)), jnp.float32)
    permittivity = jnp.clip(jnp.exp(math.log(12.0) - 2.4849066 * jax.random.uniform(streams_of[2], (NZ, NX, NY), jnp.float32) ** levels(streams_of[2], (NZ, NX, NY), ((1, 16), (2, 16)), -0.2, 0.2)), 1.0, 12.0)
    lists = choose_distinct(streams_of[3], TILES, TILES, LIST, 4096)
    mask = set_ends((jax.random.randint(streams_of[4], (TILES,), 0, 2) < 1).astype(jnp.int32), jax.random.fold_in(streams_of[4], 1), 0, 1)
    return dict(fields=fields, adjoint=adjoint, permittivity=permittivity, lists=lists, mask=mask)


TIME_STEP = 0.5
PHASE_STEP = 0.3
OMEGA = PHASE_STEP / TIME_STEP
HIGHEST = lax.Precision.HIGHEST

def ahead(field, axis):
    length = field.shape[axis]
    rest = lax.slice_in_dim(field, 1, length, axis=axis)
    edge = jnp.zeros_like(lax.slice_in_dim(field, 0, 1, axis=axis))
    return jnp.concatenate([rest, edge], axis=axis) - field

def behind(field, axis):
    length = field.shape[axis]
    rest = lax.slice_in_dim(field, 0, length - 1, axis=axis)
    edge = jnp.zeros_like(lax.slice_in_dim(field, 0, 1, axis=axis))
    return field - jnp.concatenate([edge, rest], axis=axis)

def leap_magnetic(state):
    electric_x, electric_y, electric_z = (state[0], state[1], state[2])
    magnetic_x = state[3] - TIME_STEP * (ahead(electric_z, 2) - ahead(electric_y, 0))
    magnetic_y = state[4] - TIME_STEP * (ahead(electric_x, 0) - ahead(electric_z, 1))
    magnetic_z = state[5] - TIME_STEP * (ahead(electric_y, 1) - ahead(electric_x, 2))
    return jnp.stack([electric_x, electric_y, electric_z, magnetic_x, magnetic_y, magnetic_z])

def leap_electric(state, update_scale):
    magnetic_x, magnetic_y, magnetic_z = (state[3], state[4], state[5])
    electric_x = state[0] + update_scale * (behind(magnetic_z, 2) - behind(magnetic_y, 0))
    electric_y = state[1] + update_scale * (behind(magnetic_x, 0) - behind(magnetic_z, 1))
    electric_z = state[2] + update_scale * (behind(magnetic_y, 1) - behind(magnetic_x, 2))
    return jnp.stack([electric_x, electric_y, electric_z, magnetic_x, magnetic_y, magnetic_z])

def weights_at(moment):
    theta = PHASE_STEP * moment
    return (math.cos(theta) * TIME_STEP, -math.sin(theta) * TIME_STEP)

def sweep(state, update_scale):
    shape = state.shape[1:]
    spectrum_real = jnp.zeros((3,) + shape, jnp.float32)
    spectrum_imag = jnp.zeros((3,) + shape, jnp.float32)
    plane_real = jnp.zeros((2,) + shape[1:], jnp.float32)
    plane_imag = jnp.zeros((2,) + shape[1:], jnp.float32)
    for step in (1, 2):
        state = leap_magnetic(state)
        weight_real, weight_imag = weights_at(step - 0.5)
        monitor_h = state[3:5, ZM]
        plane_real = plane_real + weight_real * monitor_h
        plane_imag = plane_imag + weight_imag * monitor_h
        state = leap_electric(state, update_scale)
        weight_real, weight_imag = weights_at(step)
        spectrum_real = spectrum_real + weight_real * state[0:3]
        spectrum_imag = spectrum_imag + weight_imag * state[0:3]
    return (state, spectrum_real, spectrum_imag, plane_real, plane_imag)

def monitor(spectrum_real, spectrum_imag, plane_real, plane_imag):
    electric_real = spectrum_real[:, ZM]
    electric_imag = spectrum_imag[:, ZM]
    return jnp.stack([-plane_real[1], plane_real[0], electric_real[1], -electric_real[0], -plane_imag[1], plane_imag[0], electric_imag[1], -electric_imag[0]])

def phase_table(index, coords, count):
    slope = (2 * index + 1 - count).astype(jnp.int32)[:, None]
    turns = slope * coords.astype(jnp.int32)[..., None, :] % (16 * count)
    angle = turns.astype(jnp.float32) * (2.0 * math.pi / (16 * count))
    return (jnp.cos(angle), jnp.sin(angle))

def rotate_rows(cosine, sine, real, imag):
    first = jnp.einsum('ux,cxy->cuy', cosine, real, precision=HIGHEST) + jnp.einsum('ux,cxy->cuy', sine, imag, precision=HIGHEST)
    second = jnp.einsum('ux,cxy->cuy', cosine, imag, precision=HIGHEST) - jnp.einsum('ux,cxy->cuy', sine, real, precision=HIGHEST)
    return (first, second)

def rotate_columns(real, imag, cosine, sine):
    first = jnp.einsum('cuy,vy->ucv', real, cosine, precision=HIGHEST) + jnp.einsum('cuy,vy->ucv', imag, sine, precision=HIGHEST)
    second = jnp.einsum('cuy,vy->ucv', imag, cosine, precision=HIGHEST) - jnp.einsum('cuy,vy->ucv', real, sine, precision=HIGHEST)
    return jnp.concatenate([first, second], axis=1)

def far_field(plane, lists, mask):
    scale = 1.0 / math.sqrt(CX * CY)
    directions = jnp.arange(DIRS_U, dtype=jnp.int32)
    anchor = jnp.zeros((), jnp.int32)

    def tile_step(carry, tile):
        tile_x = (tile // N_GY).astype(jnp.int32)
        tile_y = (tile % N_GY).astype(jnp.int32)
        piece = lax.dynamic_slice(plane, (anchor, tile_x * CX, tile_y * CY), (8, CX, CY))
        cosine, sine = phase_table(directions, tile_x * CX + jnp.arange(CX, dtype=jnp.int32), DIRS_U)
        hits = lax.optimization_barrier(jnp.sum((lists[tile][None, :] == (directions // URB)[:, None]).astype(jnp.float32), axis=1))
        hits = hits * mask[tile].astype(jnp.float32)
        part_real, part_imag = rotate_rows(cosine * hits[:, None], sine * hits[:, None], piece[:4], piece[4:])
        start = (anchor, anchor, tile_y * CY)
        old_real = lax.dynamic_slice(carry[0], start, (4, DIRS_U, CY))
        old_imag = lax.dynamic_slice(carry[1], start, (4, DIRS_U, CY))
        new_real = lax.dynamic_update_slice(carry[0], old_real + part_real, start)
        new_imag = lax.dynamic_update_slice(carry[1], old_imag + part_imag, start)
        return ((new_real, new_imag), None)
    empty = jnp.zeros((4, DIRS_U, NY), jnp.float32)
    totals, unused = lax.scan(tile_step, (empty, empty), jnp.arange(TILES, dtype=jnp.int32))
    cosine_v, sine_v = phase_table(jnp.arange(DIRS_V, dtype=jnp.int32), jnp.arange(NY, dtype=jnp.int32), DIRS_V)
    return rotate_columns(totals[0], totals[1], cosine_v, sine_v) * scale

def reference(fields, adjoint, permittivity, lists, mask):
    update_scale = TIME_STEP / permittivity
    forward = sweep(fields, update_scale)
    backward = sweep(adjoint, update_scale)
    plane = monitor(forward[1], forward[2], forward[3], forward[4])
    farfield = far_field(plane, lists, mask)
    sensitivity = OMEGA ** 2 * lax.optimization_barrier(jnp.sum(forward[1] * backward[1] - forward[2] * backward[2], axis=0))
    return (forward[0], backward[0], sensitivity, farfield)
```

```python
import functools
import math

import jax
import jax.numpy as jnp
from jax import lax
from jax.experimental import pallas as pl
from jax.experimental.pallas import tpu as pltpu
from jax.sharding import PartitionSpec as P

NZ, CX, CY = 48, 8, 128
ROWS = NZ * CX
ZM = 36
Z0 = ZM - 2
TIME_STEP = 0.5
PHASE_STEP = 0.3
OMEGA = PHASE_STEP / TIME_STEP
HIGHEST = lax.Precision.HIGHEST
MESH = pl.DeviceIdType.MESH
F32 = jnp.float32
NB = NZ // 8

ROWS_UP = [(c, 0) for c in range(6)] + [(1, 1), (2, 1), (6, 0)]
ROWS_DOWN = [(c, 7) for c in range(6)] + [(c, 6) for c in (0, 1, 2, 4, 5)] + [(6, 7)]
TILES_Y = (
    [(c, z) for c in range(3) for z in range(Z0, Z0 + 5)]
    + [(c, z) for c in range(3, 6) for z in range(Z0, Z0 + 4)]
    + [(6, z) for z in range(Z0 + 1, Z0 + 4)]
)


def weights_at(moment):
    theta = PHASE_STEP * moment
    return (math.cos(theta) * TIME_STEP, -math.sin(theta) * TIME_STEP)


def cos_turns(m):
    m = m + 512
    quarter = (m >> 10) & 3
    angle = ((m & 1023) - 512).astype(F32) * (2.0 * math.pi / 4096)
    a2 = angle * angle
    cosine = 1.0 + a2 * (-0.5 + a2 * (1 / 24 + a2 * (-1 / 720 + a2 * (1 / 40320))))
    sine = angle * (1.0 + a2 * (-1 / 6 + a2 * (1 / 120 + a2 * (-1 / 5040 + a2 * (1 / 362880)))))
    value = jnp.where((quarter & 1) == 1, sine, cosine)
    return jnp.where(((quarter + 1) & 2) == 2, -value, value)


def iota(shape, axis):
    return lax.broadcasted_iota(jnp.int32, shape, axis)


def wide(row):
    return jnp.broadcast_to(row, (8, 128))


def kernel(
    dims,
    f_ref, a_ref, eps_ref, lists_ref, mask_ref,
    fo_ref, ao_ref, sens_ref, far_ref,
    scale, xs, xr, ys, yr,
    up_s, down_s, col_s, cor_s, up_r, down_r, col_r, cor_r, dup, ddown,
    gath, wtab, vtab, tws, part, part_r, total, rows_s, rows_r,
    send_sem, recv_sem,
):
    n_zh, n_xi, n_gy = dims
    n_gx = n_zh * n_xi
    gx = lax.axis_index("gx")
    gy = lax.axis_index("gy")
    zh = gx // n_xi
    xi = gx % n_xi

    def dev(dx, dy):
        return {"gx": (gx + (dx + n_gx)) % n_gx, "gy": (gy + (dy + n_gy)) % n_gy}

    def zh_peer(d):
        return {"gx": ((zh + d) % n_zh) * n_xi + xi, "gy": gy}

    def xi_peer(d):
        return {"gx": zh * n_xi + (xi + d) % n_xi, "gy": gy}

    barrier = pltpu.get_barrier_semaphore()
    peers = [dev(dx, dy) for dx in (-1, 1) for dy in (-1, 0, 1)]
    peers += [zh_peer(d) for d in range(1, n_zh)] + [xi_peer(d) for d in range(1, n_xi)]
    for peer in peers:
        pl.semaphore_signal(barrier, inc=1, device_id=peer, device_id_type=MESH)

    def greet(d, carry):
        pl.semaphore_signal(
            barrier, inc=1, device_id={"gx": gx, "gy": (gy + d) % n_gy}, device_id_type=MESH
        )
        return carry

    lax.fori_loop(1, n_gy, greet, 0)

    started = []

    def send(src, dst, slot, peer):
        copy = pltpu.make_async_remote_copy(
            src_ref=src, dst_ref=dst, send_sem=send_sem.at[slot], recv_sem=recv_sem.at[slot],
            device_id=peer, device_id_type=MESH,
        )
        copy.start()
        started.append(copy)
        return copy

    row = iota((8, 128), 0)
    lane = iota((8, 128), 1)

    def layer(c, r, ref=f_ref):
        if c == 6:
            return eps_ref[pl.ds(Z0 * 8 + r, 8, stride=8), :]
        return ref[pl.ds(c * ROWS + Z0 * 8 + r, 8, stride=8), :]

    def tile(c, z):
        if c == 6:
            return eps_ref[z * 8 : z * 8 + 8, :]
        return f_ref[c * ROWS + z * 8 : c * ROWS + z * 8 + 8, :]

    def packed(values, low):
        out = jnp.zeros((8, 128), F32)
        for k, value in enumerate(values):
            shift = (2 * k if low else 2 * k + 2) % 128
            moved = pltpu.roll(value, shift, 1) if shift else value
            out = jnp.where((lane >> 1) == k, moved, out)
        return out

    def unpacked(low, high, k):
        first = pltpu.roll(low, (128 - 2 * k) % 128, 1) if k else low
        second = pltpu.roll(high, (126 - 2 * k) % 128, 1)
        return jnp.where(lane < 64, first, second)

    ups = [layer(c, r) for c, r in ROWS_UP]
    downs = [layer(c, r) for c, r in ROWS_DOWN]
    for k, value in enumerate(ups):
        up_s[k * 8 : k * 8 + 8, :] = value
    for k, value in enumerate(downs):
        down_s[k * 8 : k * 8 + 8, :] = value
    cor_s[0:8, :] = packed(ups, True)
    cor_s[8:16, :] = packed(ups, False)
    cor_s[16:24, :] = packed(downs, True)
    cor_s[24:32, :] = packed(downs, False)
    tiles_y = [tile(c, z) for c, z in TILES_Y]
    col_s[0:8, :] = packed(tiles_y, True)
    col_s[8:16, :] = packed(tiles_y, False)

    def at(ref, c, b, j):
        return ref[pl.ds(pl.multiple_of(c * ROWS + b * 64 + j * 8, 8), 8), :]

    def put(ref, c, b, j, value):
        ref[pl.ds(pl.multiple_of(c * ROWS + b * 64 + j * 8, 8), 8), :] = value

    def slot_of(step, state):
        return step * 2 + state

    def x_rows(ref, comps, r, slot):
        for n, c in enumerate(comps):
            xs[slot, n * NZ : n * NZ + NZ, :] = ref[pl.ds(c * ROWS + r, NZ, stride=8), :]

    def join(acc, new, b):
        moved = pltpu.roll(new, b * 8, 1)
        return jnp.where((lane >> 3) == b, moved, acc)

    def send_pair(slot, ahead):
        step = -1 if ahead else 1
        return (
            send(xs.at[slot], xr.at[slot], slot, dev(step, 0)),
            send(ys.at[slot], yr.at[slot], 8 + slot, dev(0, step)),
        )

    zero = jnp.zeros((8, 128), F32)

    def first_columns(ref, slot):
        def body(b, accs):
            out = []
            for acc, c in zip(accs, (0, 2)):
                new = zero
                for j in range(8):
                    value = at(ref, c, b, j)
                    new = jnp.where(lane == j, pltpu.roll(value, j, 1) if j else value, new)
                out.append(join(acc, new, b))
            return tuple(out)

        low, high = lax.fori_loop(0, NB, body, (zero, zero))
        ys[slot, 0:8, :] = low
        ys[slot, 8:16, :] = high

    refs_in = (f_ref, a_ref)
    refs_out = (fo_ref, ao_ref)
    for s in range(2):
        x_rows(refs_in[s], (1, 2), 0, slot_of(0, s))
        first_columns(refs_in[s], slot_of(0, s))

    pl.semaphore_wait(barrier, len(peers) + n_gy - 1)

    base = 16
    a_copies = [
        send(up_s, up_r, base + 0, dev(-1, 0)),
        send(down_s, down_r, base + 1, dev(1, 0)),
        send(col_s.at[0:8], col_r.at[0:8], base + 2, dev(0, -1)),
        send(col_s.at[8:16], col_r.at[8:16], base + 3, dev(0, 1)),
        send(cor_s.at[0:8], cor_r.at[0:8], base + 4, dev(-1, -1)),
        send(cor_s.at[8:16], cor_r.at[8:16], base + 5, dev(-1, 1)),
        send(cor_s.at[16:24], cor_r.at[16:24], base + 6, dev(1, -1)),
        send(cor_s.at[24:32], cor_r.at[24:32], base + 7, dev(1, 1)),
    ]
    pending = {}
    for s in range(2):
        pending[slot_of(0, s)] = send_pair(slot_of(0, s), True)

    def scales(b, carry):
        rows = pl.ds(pl.multiple_of(b * 64, 64), 64)
        scale[rows, :] = 0.5 / eps_ref[rows, :]
        return carry

    lax.fori_loop(0, NB, scales, 0)

    n_w = n_xi * 2 * n_gy
    n_k = n_zh * 16
    wrow = iota((n_w, 128), 0)
    wlane = iota((n_w, 128), 1)
    u = zh * (n_xi * n_gy) + (wrow // (2 * n_gy)) * n_gy + wrow % n_gy
    imag_out = (wrow // n_gy) % 2
    back = wlane // 16
    imag_in = (wlane // 8) % 2
    x = (((zh - back + n_zh) % n_zh) * n_xi + xi) * 8 + wlane % 8
    n_u = n_gx * n_gy
    weights = cos_turns((2 * u + 1 - n_u) * x * (4096 // (16 * n_u)) + 1024 * (imag_out - imag_in))
    hits = jnp.zeros((n_w, 128), F32)
    for d in range(n_zh):
        t = (((zh - d + n_zh) % n_zh) * n_xi + xi) * n_gy + gy
        same = (lists_ref[pl.ds(t, 1), :] == u[:, : lists_ref.shape[1]]).astype(F32)
        count = jnp.sum(same, axis=1, keepdims=True) * mask_ref[t].astype(F32)
        hits = jnp.where(back == d, count, hits)
    wtab[...] = weights * hits

    def v_rows(b, carry):
        y = b * 8 + iota((8, 512), 0)
        v = iota((8, 512), 1)
        vtab[pl.ds(pl.multiple_of(b * 8, 8), 8), :] = cos_turns(
            (2 * (v & 255) - 255) * y - 1024 * (v >> 8)
        )
        return carry

    lax.fori_loop(0, 16, v_rows, 0)
    d = iota((n_gy, 512), 0)
    v = iota((n_gy, 512), 1)
    tws[...] = cos_turns((2 * (v & 255) - 255) * (((gy - d + n_gy) % n_gy) * 128) - 1024 * (v >> 8))

    for copy in a_copies:
        copy.wait_recv()

    for k in range(len(ROWS_UP)):
        dup[k * 8 : k * 8 + 8, :] = unpacked(cor_r[0:8, :], cor_r[8:16, :], k)
    for k in range(len(ROWS_DOWN)):
        ddown[k * 8 : k * 8 + 8, :] = unpacked(cor_r[16:24, :], cor_r[24:32, :], k)

    far_row = gx * 8 + jnp.where(row < 4, row + 8, row - 8)
    far_lane = gy * 128 + jnp.where(lane < 64, lane + 128, lane - 128)
    row_in = (far_row >= 0) & (far_row < n_gx * 8)
    lane_in = (far_lane >= 0) & (far_lane < n_gy * 128)
    inside = [[None, lane_in], [row_in, row_in & lane_in]]
    where_up = {key: k for k, key in enumerate(ROWS_UP)}
    where_down = {key: k for k, key in enumerate(ROWS_DOWN)}

    def border_rows(up, down, c, z):
        o = z - Z0

        def get(ref, k):
            return wide(ref[k * 8 + o : k * 8 + o + 1, :])

        up0, down0 = get(up, where_up[(c, 0)]), get(down, where_down[(c, 7)])
        out = jnp.where(row < 4, up0, down0)
        if (c, 1) in where_up:
            out = jnp.where(row == 1, get(up, where_up[(c, 1)]), out)
        if (c, 6) in where_down:
            out = jnp.where(row == 6, get(down, where_down[(c, 6)]), out)
        return out

    def masked(q, other=0.0):
        return [
            [q[r][n] if inside[r][n] is None else jnp.where(inside[r][n], q[r][n], other) for n in range(2)]
            for r in range(2)
        ]

    def extended(c, z):
        k = TILES_Y.index((c, z))
        q = [
            [tile(c, z), unpacked(col_r[0:8, :], col_r[8:16, :], k)],
            [border_rows(up_r, down_r, c, z), border_rows(dup, ddown, c, z)],
        ]
        return masked(q, 1.0 if c == 6 else 0.0)

    def combine(fn, *qs):
        return [[fn(*[q[r][n] for q in qs]) for n in range(2)] for r in range(2)]

    def turn_x(q, shift, edge):
        out = [[None, None], [None, None]]
        for n in range(2):
            first, second = pltpu.roll(q[0][n], shift, 0), pltpu.roll(q[1][n], shift, 0)
            out[0][n] = jnp.where(row == edge, second, first)
            out[1][n] = jnp.where(row == edge, first, second)
        return out

    def turn_y(q, shift, edge):
        out = []
        for r in range(2):
            first, second = pltpu.roll(q[r][0], shift, 1), pltpu.roll(q[r][1], shift, 1)
            out.append([jnp.where(lane == edge, second, first), jnp.where(lane == edge, first, second)])
        return out

    def ahead_x(q):
        return combine(jnp.subtract, turn_x(q, 7, 7), q)

    def ahead_y(q):
        return combine(jnp.subtract, turn_y(q, 127, 127), q)

    def behind_x(q):
        return combine(jnp.subtract, q, turn_x(q, 1, 0))

    def behind_y(q):
        return combine(jnp.subtract, q, turn_y(q, 1, 0))

    def half(h, one, two):
        return masked(combine(lambda h, p, q: h - TIME_STEP * (p - q), h, one, two))

    def full(e, us, one, two):
        return masked(combine(lambda e, us, p, q: e + us * (p - q), e, us, one, two))

    def minus(p, q):
        return combine(jnp.subtract, p, q)

    def magnetic(e, h, zs):
        for z in zs:
            ex, ey, ez = (e[(c, z)] for c in range(3))
            h[(3, z)] = half(h[(3, z)], ahead_y(ez), minus(e[(1, z + 1)], ey))
            h[(4, z)] = half(h[(4, z)], minus(e[(0, z + 1)], ex), ahead_x(ez))
            h[(5, z)] = half(h[(5, z)], ahead_x(ey), ahead_y(ex))

    e = {(c, z): extended(c, z) for c, z in TILES_Y if c < 3}
    h = {(c, z): extended(c, z) for c, z in TILES_Y if 3 <= c < 6}
    us = {z: combine(lambda p: 0.5 / p, extended(6, z)) for c, z in TILES_Y if c == 6}
    magnetic(e, h, range(Z0, Z0 + 4))
    h1 = [h[(3, ZM)][0][0], h[(4, ZM)][0][0]]
    for z in range(Z0 + 1, Z0 + 4):
        hx, hy, hz = (h[(c, z)] for c in (3, 4, 5))
        e[(0, z)] = full(e[(0, z)], us[z], behind_y(hz), minus(hy, h[(4, z - 1)]))
        e[(1, z)] = full(e[(1, z)], us[z], minus(hx, h[(3, z - 1)]), behind_x(hz))
        e[(2, z)] = full(e[(2, z)], us[z], behind_x(hy), behind_y(hx))
    e1 = [e[(0, ZM)][0][0], e[(1, ZM)][0][0]]
    magnetic(e, h, range(Z0 + 1, Z0 + 3))
    h2 = [h[(3, ZM)][0][0], h[(4, ZM)][0][0]]
    hz = h[(5, ZM)]
    us_m = us[ZM][0][0]
    e2 = [
        e1[0] + us_m * (behind_y(hz)[0][0] - (h2[1] - h[(4, ZM - 1)][0][0])),
        e1[1] + us_m * ((h2[0] - h[(3, ZM - 1)][0][0]) - behind_x(hz)[0][0]),
    ]
    for part_of in range(2):
        first, second = weights_at(0.5)[part_of], weights_at(1.5)[part_of]
        hx, hy = (first * h1[n] + second * h2[n] for n in range(2))
        first, second = weights_at(1)[part_of], weights_at(2)[part_of]
        ex, ey = (first * e1[n] + second * e2[n] for n in range(2))
        for n, value in enumerate((-hy, hx, ey, -ex)):
            gath[0, (part_of * 4 + n) * 8 : (part_of * 4 + n) * 8 + 8, :] = value

    base_g = base + 8
    g_copies = [send(gath.at[0], gath.at[d], base_g + d - 1, zh_peer(d)) for d in range(1, n_zh)]

    def arrived(slot, ahead):
        for copy in pending[slot]:
            copy.wait_recv()
        last_x = n_gx - 1 if ahead else 0
        last_y = n_gy - 1 if ahead else 0

        @pl.when(gx == last_x)
        def _():
            xr[slot] = jnp.zeros((2 * NZ, 128), F32)

        @pl.when(gy == last_y)
        def _():
            yr[slot] = jnp.zeros((16, 128), F32)

    def magnetic_step(step, s, src, dst):
        got = slot_of(step, s)
        out = slot_of(step + 1, s)
        arrived(got, True)

        def body(b, accs):
            sides = [pltpu.roll(yr[got, n * 8 : n * 8 + 8, :], 120 - 8 * b, 1) for n in range(2)]
            news = [zero, zero]
            ex, ey, ez = (at(src, c, b, 0) for c in range(3))
            for j in range(8):
                nex, ney = at(src, 0, b, j + 1), at(src, 1, b, j + 1)
                if j == 7:
                    nex, ney = jnp.where(b < NB - 1, nex, 0.0), jnp.where(b < NB - 1, ney, 0.0)

                def along_y(value, n, j=j):
                    side = pltpu.roll(sides[n], 7 - j, 1) if j < 7 else sides[n]
                    return jnp.where(lane == 127, side, pltpu.roll(value, 127, 1)) - value

                def along_x(value, n, j=j):
                    side = wide(xr[got, pl.ds(n * NZ + b * 8 + j, 1), :])
                    return jnp.where(row == 7, side, pltpu.roll(value, 7, 0)) - value

                hx = at(src if step == 0 else dst, 3, b, j) - TIME_STEP * (along_y(ez, 1) - (ney - ey))
                hy = at(src if step == 0 else dst, 4, b, j) - TIME_STEP * ((nex - ex) - along_x(ez, 1))
                hz = at(src if step == 0 else dst, 5, b, j) - TIME_STEP * (along_x(ey, 0) - along_y(ex, 0))
                for n, value in enumerate((hx, hy, hz)):
                    put(dst, 3 + n, b, j, value)
                for n, value in enumerate((hx, hz)):
                    news[n] = jnp.where(lane == j, pltpu.roll(value, 1 + j, 1), news[n])
                if j < 7:
                    ex, ey, ez = nex, ney, at(src, 2, b, j + 1)
            return tuple(join(acc, new, b) for acc, new in zip(accs, news))

        low, high = lax.fori_loop(0, NB, body, (zero, zero))
        ys[out, 0:8, :] = low
        ys[out, 8:16, :] = high
        x_rows(dst, (4, 5), 7, out)
        pending[out] = send_pair(out, False)

    def electric_block(step, s, src, dst, b, each):
        got = slot_of(step, s)
        sides = [pltpu.roll(yr[got, n * 8 : n * 8 + 8, :], (128 - 8 * b) % 128, 1) for n in range(2)]
        phx, phy = at(dst, 3, b, -1), at(dst, 4, b, -1)
        phx, phy = jnp.where(b > 0, phx, 0.0), jnp.where(b > 0, phy, 0.0)
        for j in range(8):
            hx, hy, hz = (at(dst, c, b, j) for c in (3, 4, 5))

            def along_y(value, n, j=j):
                side = pltpu.roll(sides[n], 128 - j, 1) if j else sides[n]
                return value - jnp.where(lane == 0, side, pltpu.roll(value, 1, 1))

            def along_x(value, n, j=j):
                side = wide(xr[got, pl.ds(n * NZ + b * 8 + j, 1), :])
                return value - jnp.where(row == 0, side, pltpu.roll(value, 1, 0))

            us = at(scale, 0, b, j)
            old = [at(src, c, b, j) for c in range(3)]
            ex = old[0] + us * (along_y(hz, 1) - (hy - phy))
            ey = old[1] + us * ((hx - phx) - along_x(hz, 1))
            ez = old[2] + us * (along_x(hy, 0) - along_y(hx, 0))
            for n, value in enumerate((ex, ey, ez)):
                put(dst, n, b, j, value)
            each(j, old, [ex, ey, ez])
            phx, phy = hx, hy

    def electric_step(step, s, src, dst):
        out = slot_of(step + 1, s)
        arrived(slot_of(step, s), False)

        def body(b, accs):
            news = [zero, zero]

            def each(j, old, new):
                for n, value in enumerate((new[0], new[2])):
                    news[n] = jnp.where(lane == j, pltpu.roll(value, j, 1) if j else value, news[n])

            electric_block(step, s, src, dst, b, each)
            return tuple(join(acc, new, b) for acc, new in zip(accs, news))

        low, high = lax.fori_loop(0, NB, body, (zero, zero))
        ys[out, 0:8, :] = low
        ys[out, 8:16, :] = high
        x_rows(dst, (1, 2), 0, out)
        pending[out] = send_pair(out, True)

    def last_step():
        for s in range(2):
            arrived(slot_of(3, s), False)
        (a1, b1), (a2, b2) = weights_at(1), weights_at(2)
        k11, k12, k22 = (OMEGA**2 * k for k in (a1 * a1 - b1 * b1, a1 * a2 - b1 * b2, a2 * a2 - b2 * b2))

        def body(b, carry):
            seen = {}

            def each_forward(j, old, new):
                seen[j] = (
                    [k11 * p + k12 * q for p, q in zip(old, new)],
                    [k12 * p + k22 * q for p, q in zip(old, new)],
                )

            def each_adjoint(j, old, new):
                first, second = seen[j]
                terms = [p * w + q * z for p, q, w, z in zip(old, new, first, second)]
                put(sens_ref, 0, b, j, terms[0] + terms[1] + terms[2])

            electric_block(3, 0, fo_ref, fo_ref, b, each_forward)
            electric_block(3, 1, ao_ref, ao_ref, b, each_adjoint)
            return carry

        lax.fori_loop(0, NB, body, 0)

    for s in range(2):
        magnetic_step(0, s, refs_in[s], refs_out[s])

    for copy in g_copies:
        copy.wait_recv()
    table = wtab[:, 0:n_k]
    blk = 8 * n_gy
    for c in range(4):
        planes = jnp.concatenate(
            [gath[d, (4 * r + c) * 8 : (4 * r + c) * 8 + 8, :] for d in range(n_zh) for r in range(2)], axis=0
        )
        out = jnp.dot(table, planes, preferred_element_type=F32, precision=HIGHEST)
        for q in range(n_xi):
            for r in range(2):
                part[q * blk + r * 4 * n_gy + c * n_gy : q * blk + r * 4 * n_gy + (c + 1) * n_gy, :] = out[
                    (q * 2 + r) * n_gy : (q * 2 + r + 1) * n_gy, :
                ]
    base_r = base_g + n_zh - 1
    r_copies = []
    for d in range(1, n_xi):
        to = (xi + d) % n_xi
        r_copies.append(
            send(
                part.at[pl.ds(pl.multiple_of(to * blk, blk), blk)], part_r.at[d - 1], base_r + d - 1, xi_peer(d)
            )
        )

    for s in range(2):
        electric_step(1, s, refs_in[s], refs_out[s])

    for copy in r_copies:
        copy.wait_recv()
    acc = part[pl.ds(pl.multiple_of(xi * blk, blk), blk), :]
    for d in range(1, n_xi):
        acc = acc + part_r[d - 1]
    total[...] = acc
    for j in range(n_gy):
        rows_s[j] = total[pl.ds(j, 8, stride=n_gy), :]
    rows_r[0] = rows_s[gy]
    base_a = base_r + n_xi - 1
    last_copies = []
    for d in range(1, n_gy):
        to = (gy + d) % n_gy
        last_copies.append(
            send(rows_s.at[to], rows_r.at[d], base_a + d - 1, {"gx": gx, "gy": to})
        )

    for s in range(2):
        magnetic_step(2, s, refs_out[s], refs_out[s])

    for copy in last_copies:
        copy.wait_recv()
    turned = jnp.dot(
        rows_r[...].reshape(n_gy * 8, 128), vtab[...], preferred_element_type=F32, precision=HIGHEST
    )
    sign = jnp.where(iota((8, 256), 0) < 4, 1.0, -1.0)
    out = jnp.zeros((8, 256), F32)
    for d in range(n_gy):
        rows = turned[d * 8 : d * 8 + 8, :]
        value = rows[:, :256] + sign * pltpu.roll(rows[:, 256:], 4, 0)
        out = out + tws[d : d + 1, :256] * value + tws[d : d + 1, 256:] * (sign * pltpu.roll(value, 4, 0))
    far_ref[...] = out * (1.0 / math.sqrt(CX * CY))

    last_step()

    for copy in started:
        copy.wait_send()


def solution(mesh):
    n_gx, n_gy = mesh.shape["gx"], mesh.shape["gy"]
    n_xi = 4 if n_gx == 16 else n_gx
    dims = (n_gx // n_xi, n_xi, n_gy)
    n_zh = dims[0]
    n_sem = 16 + 8 + (n_zh - 1) + (n_xi - 1) + (n_gy - 1)
    vmem = pl.BlockSpec(memory_space=pltpu.VMEM)
    blk = 8 * n_gy

    def buffer(*shape):
        return pltpu.VMEM(shape, F32)

    def shards(fields, adjoint, permittivity, lists, mask):
        out = pl.pallas_call(
            functools.partial(kernel, dims),
            out_shape=(
                jax.ShapeDtypeStruct((6 * ROWS, 128), F32),
                jax.ShapeDtypeStruct((6 * ROWS, 128), F32),
                jax.ShapeDtypeStruct((ROWS, 128), F32),
                jax.ShapeDtypeStruct((8, 256), F32),
            ),
            in_specs=[vmem] * 4 + [pl.BlockSpec(memory_space=pltpu.SMEM)],
            out_specs=(vmem,) * 4,
            scratch_shapes=[
                buffer(ROWS, 128),
                buffer(8, 2 * NZ, 128), buffer(8, 2 * NZ, 128), buffer(8, 16, 128), buffer(8, 16, 128),
                buffer(72, 128), buffer(96, 128), buffer(16, 128), buffer(32, 128),
                buffer(72, 128), buffer(96, 128), buffer(16, 128), buffer(32, 128),
                buffer(72, 128), buffer(96, 128),
                buffer(n_zh, 64, 128), buffer(n_xi * 2 * n_gy, 128), buffer(128, 512), buffer(n_gy, 512),
                buffer(n_xi * blk, 128), buffer(max(n_xi - 1, 1), blk, 128), buffer(blk, 128),
                buffer(n_gy, 8, 128), buffer(n_gy, 8, 128),
                pltpu.SemaphoreType.DMA((n_sem,)),
                pltpu.SemaphoreType.DMA((n_sem,)),
            ],
            compiler_params=pltpu.CompilerParams(
                collective_id=0, has_side_effects=True, vmem_limit_bytes=40 * 1024 * 1024
            ),
        )(
            fields.reshape(6 * ROWS, 128),
            adjoint.reshape(6 * ROWS, 128),
            permittivity.reshape(ROWS, 128),
            lists,
            mask,
        )
        return (
            out[0].reshape(fields.shape),
            out[1].reshape(fields.shape),
            out[2].reshape(permittivity.shape),
            out[3].reshape(1, 8, 256),
        )

    in_specs = (P(None, None, "gx", "gy"), P(None, None, "gx", "gy"), P(None, "gx", "gy"), P(), P())
    out_specs = (
        P(None, None, "gx", "gy"),
        P(None, None, "gx", "gy"),
        P(None, "gx", "gy"),
        P(("gx", "gy"), None, None),
    )
    return jax.shard_map(shards, mesh=mesh, in_specs=in_specs, out_specs=out_specs, check_vma=False)
```

```python
import functools
import math

import jax
import jax.numpy as jnp
from jax import lax
from jax.experimental import pallas as pl
from jax.experimental.pallas import tpu as pltpu
from jax.sharding import PartitionSpec as P

NZ, CX, CY = 48, 8, 128
ROWS = NZ * CX
ZM = 36
Z0 = ZM - 2
TIME_STEP = 0.5
PHASE_STEP = 0.3
OMEGA = PHASE_STEP / TIME_STEP
HIGHEST = lax.Precision.HIGHEST
MESH = pl.DeviceIdType.MESH
F32 = jnp.float32
ZB = 8
NB = NZ // ZB

ROWS_UP = [(c, 0) for c in range(6)] + [(1, 1), (2, 1), (6, 0)]
ROWS_DOWN = [(c, 7) for c in range(6)] + [(c, 6) for c in (0, 1, 2, 4, 5)] + [(6, 7)]
TILES_Y = (
    [(c, z) for c in range(3) for z in range(Z0, Z0 + 5)]
    + [(c, z) for c in range(3, 6) for z in range(Z0, Z0 + 4)]
    + [(6, z) for z in range(Z0 + 1, Z0 + 4)]
)


def weights_at(moment):
    theta = PHASE_STEP * moment
    return (math.cos(theta) * TIME_STEP, -math.sin(theta) * TIME_STEP)


def cos_turns(m):
    m = m + 512
    quarter = (m >> 10) & 3
    angle = ((m & 1023) - 512).astype(F32) * (2.0 * math.pi / 4096)
    a2 = angle * angle
    cosine = 1.0 + a2 * (-0.5 + a2 * (1 / 24 + a2 * (-1 / 720 + a2 * (1 / 40320))))
    sine = angle * (1.0 + a2 * (-1 / 6 + a2 * (1 / 120 + a2 * (-1 / 5040 + a2 * (1 / 362880)))))
    value = jnp.where((quarter & 1) == 1, sine, cosine)
    return jnp.where(((quarter + 1) & 2) == 2, -value, value)


def iota(shape, axis):
    return lax.broadcasted_iota(jnp.int32, shape, axis)


def wide(row):
    return jnp.broadcast_to(row, (8, 128))


def kernel(
    dims,
    f_hbm, a_hbm, eps_hbm, lists_hbm, mask_hbm,
    fo_ref, ao_ref, sens_ref, far_ref,
    eps_ref, lists_ref, mask_ref, scale, own,
    es, er, hs, hr, ys, yr_up, yr_down, cxs, cxr, cys, cyr, hrow,
    up_s, down_s, col_s, cor_s, up_r, down_r, col_r, cor_r, dup, ddown,
    gath, wtab, vtab, tws, part, part_r, total, rows_s, rows_r,
    load_sem, send_sem, recv_sem,
):
    n_zh, n_xi, n_gy = dims
    n_gx = n_zh * n_xi
    gx = lax.axis_index("gx")
    gy = lax.axis_index("gy")
    zh = gx // n_xi
    xi = gx % n_xi

    def dev(dx, dy):
        return {"gx": (gx + (dx + n_gx)) % n_gx, "gy": (gy + (dy + n_gy)) % n_gy}

    def zh_peer(d):
        return {"gx": ((zh + d) % n_zh) * n_xi + xi, "gy": gy}

    def xi_peer(d):
        return {"gx": zh * n_xi + (xi + d) % n_xi, "gy": gy}

    barrier = pltpu.get_barrier_semaphore()
    peers = [dev(dx, dy) for dx in (-1, 1) for dy in (-1, 0, 1)]
    peers += [zh_peer(d) for d in range(1, n_zh)] + [xi_peer(d) for d in range(1, n_xi)]
    for peer in peers:
        pl.semaphore_signal(barrier, inc=1, device_id=peer, device_id_type=MESH)

    def greet(d, carry):
        pl.semaphore_signal(
            barrier, inc=1, device_id={"gx": gx, "gy": (gy + d) % n_gy}, device_id_type=MESH
        )
        return carry

    lax.fori_loop(1, n_gy, greet, 0)

    def load(src, dst, slot):
        copy = pltpu.make_async_copy(src, dst, load_sem.at[slot])
        copy.start()
        return copy

    def tile_of(d):
        return (((zh - d + n_zh) % n_zh) * n_xi + xi) * n_gy + gy

    load_f = load(f_hbm, fo_ref, 0)
    load_eps = load(eps_hbm, eps_ref, 1)
    load_a = load(a_hbm, ao_ref, 2)
    load_rest = [load(mask_hbm, mask_ref, 3)]
    for d in range(n_zh):
        first = pl.multiple_of(tile_of(d) // 8 * 8, 8)
        load_rest.append(load(lists_hbm.at[pl.ds(first, 8)], lists_ref.at[d], 4 + d))

    started = []

    def send(src, dst, slot, peer):
        copy = pltpu.make_async_remote_copy(
            src_ref=src, dst_ref=dst, send_sem=send_sem.at[slot], recv_sem=recv_sem.at[slot],
            device_id=peer, device_id_type=MESH,
        )
        copy.start()
        started.append(copy)
        return copy

    row = iota((8, 128), 0)
    lane = iota((8, 128), 1)
    zero = jnp.zeros((8, 128), F32)

    def layer(c, r):
        if c == 6:
            return eps_ref[pl.ds(Z0 * 8 + r, 8, stride=8), :]
        return fo_ref[pl.ds(c * ROWS + Z0 * 8 + r, 8, stride=8), :]

    def packed(values, low):
        out = zero
        for k, value in enumerate(values):
            shift = (2 * k if low else 2 * k + 2) % 128
            moved = pltpu.roll(value, shift, 1) if shift else value
            out = jnp.where((lane >> 1) == k, moved, out)
        return out

    def unpacked(low, high, k):
        first = pltpu.roll(low, (128 - 2 * k) % 128, 1) if k else low
        second = pltpu.roll(high, (126 - 2 * k) % 128, 1)
        return jnp.where(lane < 64, first, second)

    load_f.wait()
    load_eps.wait()
    ups = [layer(c, r) for c, r in ROWS_UP]
    downs = [layer(c, r) for c, r in ROWS_DOWN]
    for k, value in enumerate(ups):
        up_s[k * 8 : k * 8 + 8, :] = value
    for k, value in enumerate(downs):
        down_s[k * 8 : k * 8 + 8, :] = value
    cor_s[0:8, :] = packed(ups, True)
    cor_s[8:16, :] = packed(ups, False)
    cor_s[16:24, :] = packed(downs, True)
    cor_s[24:32, :] = packed(downs, False)
    tiles_y = []
    for k, (c, z) in enumerate(TILES_Y):
        at_z = z * 8 if c == 6 else c * ROWS + z * 8
        value = (eps_ref if c == 6 else fo_ref)[at_z : at_z + 8, :]
        own[k * 8 : k * 8 + 8, :] = value
        tiles_y.append(value)
    col_s[0:8, :] = packed(tiles_y, True)
    col_s[8:16, :] = packed(tiles_y, False)

    def rows_at(ref, c, r):
        return ref[pl.ds(c * ROWS + r, NZ, stride=8), :]

    def e_rows(ref, k):
        es[k, 0:NZ, :] = rows_at(ref, 1, 0)
        es[k, NZ : 2 * NZ, :] = rows_at(ref, 2, 0)

    states = (fo_ref, ao_ref)
    pending = {}

    def send_e(k):
        pending[k] = [send(es.at[k], er.at[k], k * 6, dev(-1, 0))]

    e_rows(fo_ref, 0)
    pl.semaphore_wait(barrier, len(peers) + n_gy - 1)

    base = 24
    a_copies = [
        send(up_s, up_r, base + 0, dev(-1, 0)),
        send(down_s, down_r, base + 1, dev(1, 0)),
        send(col_s.at[0:8], col_r.at[0:8], base + 2, dev(0, -1)),
        send(col_s.at[8:16], col_r.at[8:16], base + 3, dev(0, 1)),
        send(cor_s.at[0:8], cor_r.at[0:8], base + 4, dev(-1, -1)),
        send(cor_s.at[8:16], cor_r.at[8:16], base + 5, dev(-1, 1)),
        send(cor_s.at[16:24], cor_r.at[16:24], base + 6, dev(1, -1)),
        send(cor_s.at[24:32], cor_r.at[24:32], base + 7, dev(1, 1)),
    ]
    send_e(0)
    load_a.wait()
    e_rows(ao_ref, 1)
    send_e(1)

    def at(ref, c, b, j):
        return ref[pl.ds(pl.multiple_of(c * ROWS + b * (8 * ZB) + j * 8, 8), 8), :]

    def put(ref, c, b, j, value):
        ref[pl.ds(pl.multiple_of(c * ROWS + b * (8 * ZB) + j * 8, 8), 8), :] = value

    def magnetic_half(s, k):
        ref = states[s]

        def body(b, accs):
            ex = [at(ref, 0, b, j) for j in range(ZB + 1)]
            ey = [at(ref, 1, b, j) for j in range(ZB + 1)]
            ez = [at(ref, 2, b, j) for j in range(ZB)]
            old = [[at(ref, c, b, j) for j in range(ZB)] for c in (3, 4, 5)]
            ex[ZB] = jnp.where(b < NB - 1, ex[ZB], 0.0)
            ey[ZB] = jnp.where(b < NB - 1, ey[ZB], 0.0)

            def along_y(value):
                return jnp.where(lane == 127, 0.0, pltpu.roll(value, 127, 1)) - value

            def along_x(value):
                return jnp.where(row == 7, 0.0, pltpu.roll(value, 7, 0)) - value

            news = [zero, zero]
            made = []
            for j in range(ZB):
                hx = old[0][j] - TIME_STEP * (along_y(ez[j]) - (ey[j + 1] - ey[j]))
                hy = old[1][j] - TIME_STEP * ((ex[j + 1] - ex[j]) - along_x(ez[j]))
                hz = old[2][j] - TIME_STEP * (along_x(ey[j]) - along_y(ex[j]))
                made.append((hx, hy, hz))
                for n, (h, e) in enumerate(((hx, ex[j]), (hz, ez[j]))):
                    both = pltpu.roll(jnp.where(lane == 127, h, e), 2 * j + 1, 1)
                    news[n] = jnp.where((lane >> 1) == j, both, news[n])
            for j in range(ZB):
                for n in range(3):
                    put(ref, 3 + n, b, j, made[j][n])
            return tuple(
                jnp.where(lane // (2 * ZB) == b, pltpu.roll(new, b * (2 * ZB), 1), acc)
                for acc, new in zip(accs, news)
            )

        low, high = lax.fori_loop(0, NB, body, (zero, zero))
        ys[k, 0:8, :] = low
        ys[k, 8:16, :] = high
        hs[k, 0:NZ, :] = rows_at(ref, 4, 7)
        hs[k, NZ : 2 * NZ, :] = rows_at(ref, 5, 7)
        corner = zero
        for m in range(NZ // 8):
            piece = ref[pl.ds(m * 64 + 7, 8, stride=8), :]
            corner = jnp.where(lane == m, pltpu.roll(piece, m, 1) if m else piece, corner)
        cxs[k] = corner
        corner = zero
        for m in range(NZ // 8):
            piece = jnp.broadcast_to(es[k, m * 8 : m * 8 + 8, 127:128], (8, 128))
            corner = jnp.where(lane == 16 * m + 2 * row + 1, piece, corner)
        cys[k] = jnp.broadcast_to(jnp.sum(corner, axis=0, keepdims=True), (8, 128))
        pending[k] += [
            send(hs.at[k], hr.at[k], k * 6 + 1, dev(1, 0)),
            send(ys.at[k], yr_up.at[k], k * 6 + 2, dev(0, -1)),
            send(ys.at[k], yr_down.at[k], k * 6 + 3, dev(0, 1)),
            send(cxs.at[k], cxr.at[k], k * 6 + 4, dev(1, -1)),
            send(cys.at[k], cyr.at[k], k * 6 + 5, dev(-1, 1)),
        ]

    has_next_x = jnp.where(gx < n_gx - 1, 1.0, 0.0)
    has_previous_x = jnp.where(gx > 0, 1.0, 0.0)
    has_next_y = jnp.where(gy < n_gy - 1, 1.0, 0.0)
    has_previous_y = jnp.where(gy > 0, 1.0, 0.0)

    def add_rows(ref, c, value):
        ref[pl.ds(c * ROWS + 7, NZ, stride=8), :] = rows_at(ref, c, 7) + value

    def borders(s, k):
        ref = states[s]
        for copy in pending[k]:
            copy.wait_recv()
        add_rows(ref, 4, er[k, NZ : 2 * NZ, :] * (TIME_STEP * has_next_x))
        add_rows(ref, 5, er[k, 0:NZ, :] * (-TIME_STEP * has_next_x))
        hrow[k, 0:NZ, :] = (hr[k, 0:NZ, :] + TIME_STEP * es[k, NZ : 2 * NZ, :]) * has_previous_x
        for m in range(NZ // 8):
            o = m * 8
            side = jnp.where(lane == 127, pltpu.roll(cxr[k], 127 - m, 1), 0.0) * (TIME_STEP * has_next_y)
            hrow[k, NZ + o : NZ + o + 8, :] = (
                hr[k, NZ + o : NZ + o + 8, :] - TIME_STEP * es[k, o : o + 8, :] + side
            ) * has_previous_x
        corner = jnp.where(row == 7, cyr[k], 0.0) * (TIME_STEP * has_next_x)
        even = (lane & 1) == 0
        return [
            jnp.where(
                even,
                pltpu.roll(up_e, 127, 1) * (factor * has_next_y),
                (down_h + factor * own_e - other) * has_previous_y,
            )
            for up_e, down_h, own_e, factor, other in (
                (yr_up[k, 8:16, :], pltpu.roll(yr_down[k, 0:8, :], 1, 1), ys[k, 8:16, :], -TIME_STEP, zero),
                (yr_up[k, 0:8, :], pltpu.roll(yr_down[k, 8:16, :], 1, 1), ys[k, 0:8, :], TIME_STEP, corner),
            )
        ]

    def electric_block(s, k, sides, b):
        ref = states[s]
        moved = [pltpu.roll(side, 128 - b * (2 * ZB), 1) for side in sides]
        hx, hy, hz = ([at(ref, c, b, j) for j in range(-1 if c < 5 else 0, ZB)] for c in (3, 4, 5))
        hx[0] = jnp.where(b > 0, hx[0], 0.0)
        hy[0] = jnp.where(b > 0, hy[0], 0.0)
        old = [[at(ref, c, b, j) for c in range(3)] for j in range(ZB)]
        us = [at(scale, 0, b, j) for j in range(ZB)]
        behind_hx, behind_hz = [], []
        for j in range(ZB):
            for n, values, o, out in ((0, hx, j + 1, behind_hx), (1, hz, j, behind_hz)):
                side = pltpu.roll(moved[n], 127 - 2 * j, 1)
                values[o] = values[o] + jnp.where(lane == 127, side, 0.0)
                out.append(values[o] - jnp.where(lane == 0, side, pltpu.roll(values[o], 1, 1)))
        new = []
        for j in range(ZB):

            def along_x(value, n, j=j):
                side = wide(hrow[k, pl.ds(n * NZ + b * ZB + j, 1), :])
                return value - jnp.where(row == 0, side, pltpu.roll(value, 1, 0))

            new.append(
                (
                    old[j][0] + us[j] * (behind_hz[j] - (hy[j + 1] - hy[j])),
                    old[j][1] + us[j] * ((hx[j + 1] - hx[j]) - along_x(hz[j], 1)),
                    old[j][2] + us[j] * (along_x(hy[j + 1], 0) - behind_hx[j]),
                )
            )
        for j in range(ZB):
            for n in range(3):
                put(ref, n, b, j, new[j][n])
            put(ref, 3, b, j, hx[j + 1])
            put(ref, 5, b, j, hz[j])
        return old, new

    def electric_step(s, k):
        sides = borders(s, k)

        def body(b, carry):
            electric_block(s, k, sides, b)
            return carry

        lax.fori_loop(0, NB, body, 0)
        e_rows(states[s], k + 2)
        send_e(k + 2)

    def last_step():
        sides = [borders(s, 2 + s) for s in range(2)]
        (a1, b1), (a2, b2) = weights_at(1), weights_at(2)
        k11, k12, k22 = (OMEGA**2 * k for k in (a1 * a1 - b1 * b1, a1 * a2 - b1 * b2, a2 * a2 - b2 * b2))

        def body(b, carry):
            f_old, f_new = electric_block(0, 2, sides[0], b)
            first = [[k11 * p + k12 * q for p, q in zip(*pair)] for pair in zip(f_old, f_new)]
            second = [[k12 * p + k22 * q for p, q in zip(*pair)] for pair in zip(f_old, f_new)]
            a_old, a_new = electric_block(1, 3, sides[1], b)
            for j in range(ZB):
                terms = [a_old[j][n] * first[j][n] + a_new[j][n] * second[j][n] for n in range(3)]
                put(sens_ref, 0, b, j, terms[0] + terms[1] + terms[2])
            return carry

        lax.fori_loop(0, NB, body, 0)

    for s in range(2):
        magnetic_half(s, s)

    def scales(b, carry):
        rows = pl.ds(pl.multiple_of(b * 64, 64), 64)
        scale[rows, :] = 0.5 / eps_ref[rows, :]
        return carry

    lax.fori_loop(0, ROWS // 64, scales, 0)

    for copy in a_copies:
        copy.wait_recv()

    for k in range(len(ROWS_UP)):
        dup[k * 8 : k * 8 + 8, :] = unpacked(cor_r[0:8, :], cor_r[8:16, :], k)
    for k in range(len(ROWS_DOWN)):
        ddown[k * 8 : k * 8 + 8, :] = unpacked(cor_r[16:24, :], cor_r[24:32, :], k)

    far_row = gx * 8 + jnp.where(row < 4, row + 8, row - 8)
    far_lane = gy * 128 + jnp.where(lane < 64, lane + 128, lane - 128)
    row_in = (far_row >= 0) & (far_row < n_gx * 8)
    lane_in = (far_lane >= 0) & (far_lane < n_gy * 128)
    inside = [[None, lane_in], [row_in, row_in & lane_in]]
    where_up = {key: k for k, key in enumerate(ROWS_UP)}
    where_down = {key: k for k, key in enumerate(ROWS_DOWN)}

    def border_rows(up, down, c, z):
        o = z - Z0

        def get(ref, k):
            return wide(ref[k * 8 + o : k * 8 + o + 1, :])

        up0, down0 = get(up, where_up[(c, 0)]), get(down, where_down[(c, 7)])
        out = jnp.where(row < 4, up0, down0)
        if (c, 1) in where_up:
            out = jnp.where(row == 1, get(up, where_up[(c, 1)]), out)
        if (c, 6) in where_down:
            out = jnp.where(row == 6, get(down, where_down[(c, 6)]), out)
        return out

    def masked(q, other=0.0):
        return [
            [q[r][n] if inside[r][n] is None else jnp.where(inside[r][n], q[r][n], other) for n in range(2)]
            for r in range(2)
        ]

    def extended(c, z):
        k = TILES_Y.index((c, z))
        q = [
            [own[k * 8 : k * 8 + 8, :], unpacked(col_r[0:8, :], col_r[8:16, :], k)],
            [border_rows(up_r, down_r, c, z), border_rows(dup, ddown, c, z)],
        ]
        return masked(q, 1.0 if c == 6 else 0.0)

    def combine(fn, *qs):
        return [[fn(*[q[r][n] for q in qs]) for n in range(2)] for r in range(2)]

    def turn_x(q, shift, edge):
        out = [[None, None], [None, None]]
        for n in range(2):
            first, second = pltpu.roll(q[0][n], shift, 0), pltpu.roll(q[1][n], shift, 0)
            out[0][n] = jnp.where(row == edge, second, first)
            out[1][n] = jnp.where(row == edge, first, second)
        return out

    def turn_y(q, shift, edge):
        out = []
        for r in range(2):
            first, second = pltpu.roll(q[r][0], shift, 1), pltpu.roll(q[r][1], shift, 1)
            out.append([jnp.where(lane == edge, second, first), jnp.where(lane == edge, first, second)])
        return out

    def ahead_x(q):
        return combine(jnp.subtract, turn_x(q, 7, 7), q)

    def ahead_y(q):
        return combine(jnp.subtract, turn_y(q, 127, 127), q)

    def behind_x(q):
        return combine(jnp.subtract, q, turn_x(q, 1, 0))

    def behind_y(q):
        return combine(jnp.subtract, q, turn_y(q, 1, 0))

    def half(h, one, two):
        return masked(combine(lambda h, p, q: h - TIME_STEP * (p - q), h, one, two))

    def full(e, us, one, two):
        return masked(combine(lambda e, us, p, q: e + us * (p - q), e, us, one, two))

    def minus(p, q):
        return combine(jnp.subtract, p, q)

    def magnetic(e, h, zs):
        for z in zs:
            ex, ey, ez = (e[(c, z)] for c in range(3))
            h[(3, z)] = half(h[(3, z)], ahead_y(ez), minus(e[(1, z + 1)], ey))
            h[(4, z)] = half(h[(4, z)], minus(e[(0, z + 1)], ex), ahead_x(ez))
            h[(5, z)] = half(h[(5, z)], ahead_x(ey), ahead_y(ex))

    e = {(c, z): extended(c, z) for c, z in TILES_Y if c < 3}
    h = {(c, z): extended(c, z) for c, z in TILES_Y if 3 <= c < 6}
    us = {z: combine(lambda p: 0.5 / p, extended(6, z)) for c, z in TILES_Y if c == 6}
    magnetic(e, h, range(Z0, Z0 + 4))
    h1 = [h[(3, ZM)][0][0], h[(4, ZM)][0][0]]
    for z in range(Z0 + 1, Z0 + 4):
        hx, hy, hz = (h[(c, z)] for c in (3, 4, 5))
        e[(0, z)] = full(e[(0, z)], us[z], behind_y(hz), minus(hy, h[(4, z - 1)]))
        e[(1, z)] = full(e[(1, z)], us[z], minus(hx, h[(3, z - 1)]), behind_x(hz))
        e[(2, z)] = full(e[(2, z)], us[z], behind_x(hy), behind_y(hx))
    e1 = [e[(0, ZM)][0][0], e[(1, ZM)][0][0]]
    magnetic(e, h, range(Z0 + 1, Z0 + 3))
    h2 = [h[(3, ZM)][0][0], h[(4, ZM)][0][0]]
    hz = h[(5, ZM)]
    us_m = us[ZM][0][0]
    e2 = [
        e1[0] + us_m * (behind_y(hz)[0][0] - (h2[1] - h[(4, ZM - 1)][0][0])),
        e1[1] + us_m * ((h2[0] - h[(3, ZM - 1)][0][0]) - behind_x(hz)[0][0]),
    ]
    for part_of in range(2):
        first, second = weights_at(0.5)[part_of], weights_at(1.5)[part_of]
        hx, hy = (first * h1[n] + second * h2[n] for n in range(2))
        first, second = weights_at(1)[part_of], weights_at(2)[part_of]
        ex, ey = (first * e1[n] + second * e2[n] for n in range(2))
        for n, value in enumerate((-hy, hx, ey, -ex)):
            gath[0, (part_of * 4 + n) * 8 : (part_of * 4 + n) * 8 + 8, :] = value

    base_g = base + 8
    g_copies = [send(gath.at[0], gath.at[d], base_g + d - 1, zh_peer(d)) for d in range(1, n_zh)]

    for copy in load_rest:
        copy.wait()
    n_w = n_xi * 2 * n_gy
    n_k = n_zh * 16
    wrow = iota((n_w, 128), 0)
    wlane = iota((n_w, 128), 1)
    u = zh * (n_xi * n_gy) + (wrow // (2 * n_gy)) * n_gy + wrow % n_gy
    imag_out = (wrow // n_gy) % 2
    back = wlane // 16
    imag_in = (wlane // 8) % 2
    x = (((zh - back + n_zh) % n_zh) * n_xi + xi) * 8 + wlane % 8
    n_u = n_gx * n_gy
    weights = cos_turns((2 * u + 1 - n_u) * x * (4096 // (16 * n_u)) + 1024 * (imag_out - imag_in))
    hits = jnp.zeros((n_w, 128), F32)
    for d in range(n_zh):
        t = tile_of(d)
        same = (lists_ref[d, pl.ds(t % 8, 1), :] == u[:, : lists_ref.shape[2]]).astype(F32)
        count = jnp.sum(same, axis=1, keepdims=True) * mask_ref[t].astype(F32)
        hits = jnp.where(back == d, count, hits)
    wtab[...] = weights * hits

    def v_rows(b, carry):
        y = b * 8 + iota((8, 512), 0)
        v = iota((8, 512), 1)
        vtab[pl.ds(pl.multiple_of(b * 8, 8), 8), :] = cos_turns(
            (2 * (v & 255) - 255) * y - 1024 * (v >> 8)
        )
        return carry

    lax.fori_loop(0, 16, v_rows, 0)
    d = iota((n_gy, 512), 0)
    v = iota((n_gy, 512), 1)
    tws[...] = cos_turns((2 * (v & 255) - 255) * (((gy - d + n_gy) % n_gy) * 128) - 1024 * (v >> 8))

    electric_step(0, 0)
    magnetic_half(0, 2)

    for copy in g_copies:
        copy.wait_recv()
    table = wtab[:, 0:n_k]
    blk = 8 * n_gy
    for c in range(4):
        planes = jnp.concatenate(
            [gath[d, (4 * r + c) * 8 : (4 * r + c) * 8 + 8, :] for d in range(n_zh) for r in range(2)], axis=0
        )
        out = jnp.dot(table, planes, preferred_element_type=F32, precision=HIGHEST)
        for q in range(n_xi):
            for r in range(2):
                part[q * blk + r * 4 * n_gy + c * n_gy : q * blk + r * 4 * n_gy + (c + 1) * n_gy, :] = out[
                    (q * 2 + r) * n_gy : (q * 2 + r + 1) * n_gy, :
                ]
    base_r = base_g + n_zh - 1
    r_copies = []
    for d in range(1, n_xi):
        to = (xi + d) % n_xi
        r_copies.append(
            send(
                part.at[pl.ds(pl.multiple_of(to * blk, blk), blk)], part_r.at[d - 1], base_r + d - 1, xi_peer(d)
            )
        )

    electric_step(1, 1)
    magnetic_half(1, 3)

    for copy in r_copies:
        copy.wait_recv()
    acc = part[pl.ds(pl.multiple_of(xi * blk, blk), blk), :]
    for d in range(1, n_xi):
        acc = acc + part_r[d - 1]
    total[...] = acc
    for j in range(n_gy):
        rows_s[j] = total[pl.ds(j, 8, stride=n_gy), :]
    rows_r[0] = rows_s[gy]
    base_a = base_r + n_xi - 1
    last_copies = []
    for d in range(1, n_gy):
        to = (gy + d) % n_gy
        last_copies.append(
            send(rows_s.at[to], rows_r.at[d], base_a + d - 1, {"gx": gx, "gy": to})
        )

    last_step()

    for copy in last_copies:
        copy.wait_recv()
    turned = jnp.dot(
        rows_r[...].reshape(n_gy * 8, 128), vtab[...], preferred_element_type=F32, precision=HIGHEST
    )
    sign = jnp.where(iota((8, 256), 0) < 4, 1.0, -1.0)
    out = jnp.zeros((8, 256), F32)
    for d in range(n_gy):
        rows = turned[d * 8 : d * 8 + 8, :]
        value = rows[:, :256] + sign * pltpu.roll(rows[:, 256:], 4, 0)
        out = out + tws[d : d + 1, :256] * value + tws[d : d + 1, 256:] * (sign * pltpu.roll(value, 4, 0))
    far_ref[...] = out * (1.0 / math.sqrt(CX * CY))

    for copy in started:
        copy.wait_send()


def write_out(*refs):
    n = len(refs) // 2
    sems = refs[-1]
    copies = [pltpu.make_async_copy(refs[i], refs[n + i], sems.at[i]) for i in range(n)]
    for copy in copies:
        copy.start()
    for copy in copies:
        copy.wait()


def solution(mesh):
    n_gx, n_gy = mesh.shape["gx"], mesh.shape["gy"]
    n_xi = 4 if n_gx == 16 else n_gx
    dims = (n_gx // n_xi, n_xi, n_gy)
    n_zh = dims[0]
    n_sem = 24 + 8 + (n_zh - 1) + (n_xi - 1) + (n_gy - 1)
    vmem = pl.BlockSpec(memory_space=pltpu.VMEM)
    hbm = pl.BlockSpec(memory_space=pltpu.HBM)
    blk = 8 * n_gy

    def buffer(*shape):
        return pltpu.VMEM(shape, F32)

    def shards(fields, adjoint, permittivity, lists, mask):
        shapes = (
            jax.ShapeDtypeStruct((6 * ROWS, 128), F32),
            jax.ShapeDtypeStruct((6 * ROWS, 128), F32),
            jax.ShapeDtypeStruct((ROWS, 128), F32),
            jax.ShapeDtypeStruct((8, 256), F32),
        )
        made = pl.pallas_call(
            functools.partial(kernel, dims),
            out_shape=shapes,
            in_specs=[hbm] * 5,
            out_specs=(vmem,) * 4,
            scratch_shapes=[
                buffer(ROWS, 128),
                pltpu.VMEM((n_zh, 8, lists.shape[1]), jnp.int32),
                pltpu.SMEM(mask.shape, jnp.int32),
                buffer(ROWS, 128),
                buffer(8 * len(TILES_Y), 128),
                buffer(4, 2 * NZ, 128), buffer(4, 2 * NZ, 128), buffer(4, 2 * NZ, 128), buffer(4, 2 * NZ, 128),
                buffer(4, 16, 128), buffer(4, 16, 128), buffer(4, 16, 128),
                buffer(4, 8, 128), buffer(4, 8, 128), buffer(4, 8, 128), buffer(4, 8, 128),
                buffer(4, 2 * NZ, 128),
                buffer(72, 128), buffer(96, 128), buffer(16, 128), buffer(32, 128),
                buffer(72, 128), buffer(96, 128), buffer(16, 128), buffer(32, 128),
                buffer(72, 128), buffer(96, 128),
                buffer(n_zh, 64, 128), buffer(n_xi * 2 * n_gy, 128), buffer(128, 512), buffer(n_gy, 512),
                buffer(n_xi * blk, 128), buffer(max(n_xi - 1, 1), blk, 128), buffer(blk, 128),
                buffer(n_gy, 8, 128), buffer(n_gy, 8, 128),
                pltpu.SemaphoreType.DMA((4 + n_zh,)),
                pltpu.SemaphoreType.DMA((n_sem,)),
                pltpu.SemaphoreType.DMA((n_sem,)),
            ],
            compiler_params=pltpu.CompilerParams(
                collective_id=0, has_side_effects=True, vmem_limit_bytes=58 * 1024 * 1024
            ),
        )(
            fields.reshape(6 * ROWS, 128),
            adjoint.reshape(6 * ROWS, 128),
            permittivity.reshape(ROWS, 128),
            lists,
            mask,
        )
        out = pl.pallas_call(
            write_out,
            out_shape=shapes,
            in_specs=[vmem] * 4,
            out_specs=(pl.BlockSpec(memory_space=pl.ANY),) * 4,
            scratch_shapes=[pltpu.SemaphoreType.DMA((4,))],
        )(*made)
        return (
            out[0].reshape(fields.shape),
            out[1].reshape(fields.shape),
            out[2].reshape(permittivity.shape),
            out[3].reshape(1, 8, 256),
        )

    in_specs = (P(None, None, "gx", "gy"), P(None, None, "gx", "gy"), P(None, "gx", "gy"), P(), P())
    out_specs = (
        P(None, None, "gx", "gy"),
        P(None, None, "gx", "gy"),
        P(None, "gx", "gy"),
        P(("gx", "gy"), None, None),
    )
    return jax.shard_map(shards, mesh=mesh, in_specs=in_specs, out_specs=out_specs, check_vma=False)
```

```python
import functools
import math

import jax
import jax.numpy as jnp
from jax import lax
from jax.experimental import pallas as pl
from jax.experimental.pallas import tpu as pltpu
from jax.sharding import PartitionSpec as P

NZ, CX, CY = 48, 8, 128
ROWS = NZ * CX
ZM = 36
Z0 = ZM - 2
TIME_STEP = 0.5
PHASE_STEP = 0.3
OMEGA = PHASE_STEP / TIME_STEP
HIGHEST = lax.Precision.HIGHEST
MESH = pl.DeviceIdType.MESH
F32 = jnp.float32
ZB = 24
NB = NZ // ZB

ROWS_UP = [(c, 0) for c in range(6)] + [(1, 1), (2, 1), (6, 0)]
ROWS_DOWN = [(c, 7) for c in range(6)] + [(c, 6) for c in (0, 1, 2, 4, 5)] + [(6, 7)]
TILES_Y = (
    [(c, z) for c in range(3) for z in range(Z0, Z0 + 5)]
    + [(c, z) for c in range(3, 6) for z in range(Z0, Z0 + 4)]
    + [(6, z) for z in range(Z0 + 1, Z0 + 4)]
)


def weights_at(moment):
    theta = PHASE_STEP * moment
    return (math.cos(theta) * TIME_STEP, -math.sin(theta) * TIME_STEP)


def cos_turns(m):
    m = m + 512
    quarter = (m >> 10) & 3
    angle = ((m & 1023) - 512).astype(F32) * (2.0 * math.pi / 4096)
    a2 = angle * angle
    cosine = 1.0 + a2 * (-0.5 + a2 * (1 / 24 + a2 * (-1 / 720 + a2 * (1 / 40320))))
    sine = angle * (1.0 + a2 * (-1 / 6 + a2 * (1 / 120 + a2 * (-1 / 5040 + a2 * (1 / 362880)))))
    value = jnp.where((quarter & 1) == 1, sine, cosine)
    return jnp.where(((quarter + 1) & 2) == 2, -value, value)


def iota(shape, axis):
    return lax.broadcasted_iota(jnp.int32, shape, axis)


def wide(row):
    return jnp.broadcast_to(row, (8, 128))


def kernel(
    dims,
    f_hbm, a_hbm, eps_hbm, lists_hbm, mask_hbm,
    fo_ref, ao_ref, sens_ref, far_ref,
    eps_ref, lists_ref, mask_ref, scale, own,
    es, er, hs, hr, ys, yr_up, yr_down, cxs, cxr, cys, cyr, hrow,
    up_s, down_s, col_s, cor_s, up_r, down_r, col_r, cor_r, dup, ddown,
    gath, wtab, vtab, tws, part, part_r, total, rows_s, rows_r,
    load_sem, send_sem, recv_sem,
):
    n_zh, n_xi, n_gy = dims
    n_gx = n_zh * n_xi
    gx = lax.axis_index("gx")
    gy = lax.axis_index("gy")
    zh = gx // n_xi
    xi = gx % n_xi

    def dev(dx, dy):
        return {"gx": (gx + (dx + n_gx)) % n_gx, "gy": (gy + (dy + n_gy)) % n_gy}

    def zh_peer(d):
        return {"gx": ((zh + d) % n_zh) * n_xi + xi, "gy": gy}

    def xi_peer(d):
        return {"gx": zh * n_xi + (xi + d) % n_xi, "gy": gy}

    barrier = pltpu.get_barrier_semaphore()
    peers = [dev(dx, dy) for dx in (-1, 1) for dy in (-1, 0, 1)]
    peers += [zh_peer(d) for d in range(1, n_zh)] + [xi_peer(d) for d in range(1, n_xi)]
    for peer in peers:
        pl.semaphore_signal(barrier, inc=1, device_id=peer, device_id_type=MESH)

    def greet(d, carry):
        pl.semaphore_signal(
            barrier, inc=1, device_id={"gx": gx, "gy": (gy + d) % n_gy}, device_id_type=MESH
        )
        return carry

    lax.fori_loop(1, n_gy, greet, 0)

    def load(src, dst, slot):
        copy = pltpu.make_async_copy(src, dst, load_sem.at[slot])
        copy.start()
        return copy

    def tile_of(d):
        return (((zh - d + n_zh) % n_zh) * n_xi + xi) * n_gy + gy

    load_f = load(f_hbm, fo_ref, 0)
    load_eps = load(eps_hbm, eps_ref, 1)
    load_a = load(a_hbm, ao_ref, 2)
    load_rest = [load(mask_hbm, mask_ref, 3)]
    for d in range(n_zh):
        first = pl.multiple_of(tile_of(d) // 8 * 8, 8)
        load_rest.append(load(lists_hbm.at[pl.ds(first, 8)], lists_ref.at[d], 4 + d))

    started = []

    def send(src, dst, slot, peer):
        copy = pltpu.make_async_remote_copy(
            src_ref=src, dst_ref=dst, send_sem=send_sem.at[slot], recv_sem=recv_sem.at[slot],
            device_id=peer, device_id_type=MESH,
        )
        copy.start()
        started.append(copy)
        return copy

    row = iota((8, 128), 0)
    lane = iota((8, 128), 1)
    zero = jnp.zeros((8, 128), F32)

    def layer(c, r):
        if c == 6:
            return eps_ref[pl.ds(Z0 * 8 + r, 8, stride=8), :]
        return fo_ref[pl.ds(c * ROWS + Z0 * 8 + r, 8, stride=8), :]

    def packed(values, low):
        out = zero
        for k, value in enumerate(values):
            shift = (2 * k if low else 2 * k + 2) % 128
            moved = pltpu.roll(value, shift, 1) if shift else value
            out = jnp.where((lane >> 1) == k, moved, out)
        return out

    def unpacked(low, high, k):
        first = pltpu.roll(low, (128 - 2 * k) % 128, 1) if k else low
        second = pltpu.roll(high, (126 - 2 * k) % 128, 1)
        return jnp.where(lane < 64, first, second)

    load_f.wait()
    load_eps.wait()
    ups = [layer(c, r) for c, r in ROWS_UP]
    downs = [layer(c, r) for c, r in ROWS_DOWN]
    for k, value in enumerate(ups):
        up_s[k * 8 : k * 8 + 8, :] = value
    for k, value in enumerate(downs):
        down_s[k * 8 : k * 8 + 8, :] = value
    cor_s[0:8, :] = packed(ups, True)
    cor_s[8:16, :] = packed(ups, False)
    cor_s[16:24, :] = packed(downs, True)
    cor_s[24:32, :] = packed(downs, False)
    tiles_y = []
    for k, (c, z) in enumerate(TILES_Y):
        at_z = z * 8 if c == 6 else c * ROWS + z * 8
        value = (eps_ref if c == 6 else fo_ref)[at_z : at_z + 8, :]
        own[k * 8 : k * 8 + 8, :] = value
        tiles_y.append(value)
    col_s[0:8, :] = packed(tiles_y, True)
    col_s[8:16, :] = packed(tiles_y, False)

    def rows_at(ref, c, r):
        return ref[pl.ds(c * ROWS + r, NZ, stride=8), :]

    def e_rows(ref, k):
        es[k, 0:NZ, :] = rows_at(ref, 1, 0)
        es[k, NZ : 2 * NZ, :] = rows_at(ref, 2, 0)

    states = (fo_ref, ao_ref)
    pending = {}

    def send_e(k):
        pending[k] = [send(es.at[k], er.at[k], k * 6, dev(-1, 0))]

    e_rows(fo_ref, 0)
    pl.semaphore_wait(barrier, len(peers) + n_gy - 1)

    base = 24
    a_copies = [
        send(up_s, up_r, base + 0, dev(-1, 0)),
        send(down_s, down_r, base + 1, dev(1, 0)),
        send(col_s.at[0:8], col_r.at[0:8], base + 2, dev(0, -1)),
        send(col_s.at[8:16], col_r.at[8:16], base + 3, dev(0, 1)),
        send(cor_s.at[0:8], cor_r.at[0:8], base + 4, dev(-1, -1)),
        send(cor_s.at[8:16], cor_r.at[8:16], base + 5, dev(-1, 1)),
        send(cor_s.at[16:24], cor_r.at[16:24], base + 6, dev(1, -1)),
        send(cor_s.at[24:32], cor_r.at[24:32], base + 7, dev(1, 1)),
    ]
    send_e(0)
    load_a.wait()
    e_rows(ao_ref, 1)
    send_e(1)

    def at(ref, c, b, j):
        return ref[pl.ds(pl.multiple_of(c * ROWS + b * (8 * ZB) + j * 8, 8), 8), :]

    def put(ref, c, b, j, value):
        ref[pl.ds(pl.multiple_of(c * ROWS + b * (8 * ZB) + j * 8, 8), 8), :] = value

    def magnetic_half(s, k):
        ref = states[s]

        def body(b, accs):
            ex = [at(ref, 0, b, j) for j in range(ZB + 1)]
            ey = [at(ref, 1, b, j) for j in range(ZB + 1)]
            ez = [at(ref, 2, b, j) for j in range(ZB)]
            old = [[at(ref, c, b, j) for j in range(ZB)] for c in (3, 4, 5)]
            ex[ZB] = jnp.where(b < NB - 1, ex[ZB], 0.0)
            ey[ZB] = jnp.where(b < NB - 1, ey[ZB], 0.0)

            def along_y(value):
                return jnp.where(lane == 127, 0.0, pltpu.roll(value, 127, 1)) - value

            def along_x(value):
                return jnp.where(row == 7, 0.0, pltpu.roll(value, 7, 0)) - value

            news = [zero, zero]
            made = []
            for j in range(ZB):
                hx = old[0][j] - TIME_STEP * (along_y(ez[j]) - (ey[j + 1] - ey[j]))
                hy = old[1][j] - TIME_STEP * ((ex[j + 1] - ex[j]) - along_x(ez[j]))
                hz = old[2][j] - TIME_STEP * (along_x(ey[j]) - along_y(ex[j]))
                made.append((hx, hy, hz))
                for n, (h, e) in enumerate(((hx, ex[j]), (hz, ez[j]))):
                    both = pltpu.roll(jnp.where(lane == 127, h, e), 2 * j + 1, 1)
                    news[n] = jnp.where((lane >> 1) == j, both, news[n])
            for j in range(ZB):
                for n in range(3):
                    put(ref, 3 + n, b, j, made[j][n])
            return tuple(
                jnp.where(lane // (2 * ZB) == b, pltpu.roll(new, b * (2 * ZB), 1), acc)
                for acc, new in zip(accs, news)
            )

        low, high = lax.fori_loop(0, NB, body, (zero, zero))
        ys[k, 0:8, :] = low
        ys[k, 8:16, :] = high
        hs[k, 0:NZ, :] = rows_at(ref, 4, 7)
        hs[k, NZ : 2 * NZ, :] = rows_at(ref, 5, 7)
        corner = zero
        for m in range(NZ // 8):
            piece = ref[pl.ds(m * 64 + 7, 8, stride=8), :]
            corner = jnp.where(lane == m, pltpu.roll(piece, m, 1) if m else piece, corner)
        cxs[k] = corner
        corner = zero
        for m in range(NZ // 8):
            piece = jnp.broadcast_to(es[k, m * 8 : m * 8 + 8, 127:128], (8, 128))
            corner = jnp.where(lane == 16 * m + 2 * row + 1, piece, corner)
        cys[k] = jnp.broadcast_to(jnp.sum(corner, axis=0, keepdims=True), (8, 128))
        pending[k] += [
            send(hs.at[k], hr.at[k], k * 6 + 1, dev(1, 0)),
            send(ys.at[k], yr_up.at[k], k * 6 + 2, dev(0, -1)),
            send(ys.at[k], yr_down.at[k], k * 6 + 3, dev(0, 1)),
            send(cxs.at[k], cxr.at[k], k * 6 + 4, dev(1, -1)),
            send(cys.at[k], cyr.at[k], k * 6 + 5, dev(-1, 1)),
        ]

    has_next_x = jnp.where(gx < n_gx - 1, 1.0, 0.0)
    has_previous_x = jnp.where(gx > 0, 1.0, 0.0)
    has_next_y = jnp.where(gy < n_gy - 1, 1.0, 0.0)
    has_previous_y = jnp.where(gy > 0, 1.0, 0.0)

    def add_rows(ref, c, value):
        ref[pl.ds(c * ROWS + 7, NZ, stride=8), :] = rows_at(ref, c, 7) + value

    def borders(s, k):
        ref = states[s]
        for copy in pending[k]:
            copy.wait_recv()
        add_rows(ref, 4, er[k, NZ : 2 * NZ, :] * (TIME_STEP * has_next_x))
        add_rows(ref, 5, er[k, 0:NZ, :] * (-TIME_STEP * has_next_x))
        hrow[k, 0:NZ, :] = (hr[k, 0:NZ, :] + TIME_STEP * es[k, NZ : 2 * NZ, :]) * has_previous_x
        for m in range(NZ // 8):
            o = m * 8
            side = jnp.where(lane == 127, pltpu.roll(cxr[k], 127 - m, 1), 0.0) * (TIME_STEP * has_next_y)
            hrow[k, NZ + o : NZ + o + 8, :] = (
                hr[k, NZ + o : NZ + o + 8, :] - TIME_STEP * es[k, o : o + 8, :] + side
            ) * has_previous_x
        corner = jnp.where(row == 7, cyr[k], 0.0) * (TIME_STEP * has_next_x)
        even = (lane & 1) == 0
        return [
            jnp.where(
                even,
                pltpu.roll(up_e, 127, 1) * (factor * has_next_y),
                (down_h + factor * own_e - other) * has_previous_y,
            )
            for up_e, down_h, own_e, factor, other in (
                (yr_up[k, 8:16, :], pltpu.roll(yr_down[k, 0:8, :], 1, 1), ys[k, 8:16, :], -TIME_STEP, zero),
                (yr_up[k, 0:8, :], pltpu.roll(yr_down[k, 8:16, :], 1, 1), ys[k, 0:8, :], TIME_STEP, corner),
            )
        ]

    def electric_block(s, k, sides, b):
        ref = states[s]
        moved = [pltpu.roll(side, 128 - b * (2 * ZB), 1) for side in sides]
        hx, hy, hz = ([at(ref, c, b, j) for j in range(-1 if c < 5 else 0, ZB)] for c in (3, 4, 5))
        hx[0] = jnp.where(b > 0, hx[0], 0.0)
        hy[0] = jnp.where(b > 0, hy[0], 0.0)
        old = [[at(ref, c, b, j) for c in range(3)] for j in range(ZB)]
        us = [at(scale, 0, b, j) for j in range(ZB)]
        behind_hx, behind_hz = [], []
        for j in range(ZB):
            for n, values, o, out in ((0, hx, j + 1, behind_hx), (1, hz, j, behind_hz)):
                side = pltpu.roll(moved[n], 127 - 2 * j, 1)
                values[o] = values[o] + jnp.where(lane == 127, side, 0.0)
                out.append(values[o] - jnp.where(lane == 0, side, pltpu.roll(values[o], 1, 1)))
        new = []
        for j in range(ZB):

            def along_x(value, n, j=j):
                side = wide(hrow[k, pl.ds(n * NZ + b * ZB + j, 1), :])
                return value - jnp.where(row == 0, side, pltpu.roll(value, 1, 0))

            new.append(
                (
                    old[j][0] + us[j] * (behind_hz[j] - (hy[j + 1] - hy[j])),
                    old[j][1] + us[j] * ((hx[j + 1] - hx[j]) - along_x(hz[j], 1)),
                    old[j][2] + us[j] * (along_x(hy[j + 1], 0) - behind_hx[j]),
                )
            )
        for j in range(ZB):
            for n in range(3):
                put(ref, n, b, j, new[j][n])
            put(ref, 3, b, j, hx[j + 1])
            put(ref, 5, b, j, hz[j])
        return old, new

    def electric_step(s, k):
        sides = borders(s, k)

        def body(b, carry):
            electric_block(s, k, sides, b)
            return carry

        lax.fori_loop(0, NB, body, 0)
        e_rows(states[s], k + 2)
        send_e(k + 2)

    def last_step():
        sides = [borders(s, 2 + s) for s in range(2)]
        (a1, b1), (a2, b2) = weights_at(1), weights_at(2)
        k11, k12, k22 = (OMEGA**2 * k for k in (a1 * a1 - b1 * b1, a1 * a2 - b1 * b2, a2 * a2 - b2 * b2))

        def body(b, carry):
            f_old, f_new = electric_block(0, 2, sides[0], b)
            first = [[k11 * p + k12 * q for p, q in zip(*pair)] for pair in zip(f_old, f_new)]
            second = [[k12 * p + k22 * q for p, q in zip(*pair)] for pair in zip(f_old, f_new)]
            a_old, a_new = electric_block(1, 3, sides[1], b)
            for j in range(ZB):
                terms = [a_old[j][n] * first[j][n] + a_new[j][n] * second[j][n] for n in range(3)]
                put(sens_ref, 0, b, j, terms[0] + terms[1] + terms[2])
            return carry

        lax.fori_loop(0, NB, body, 0)

    for s in range(2):
        magnetic_half(s, s)

    def scales(b, carry):
        rows = pl.ds(pl.multiple_of(b * 192, 192), 192)
        scale[rows, :] = 0.5 / eps_ref[rows, :]
        return carry

    lax.fori_loop(0, ROWS // 192, scales, 0)

    for copy in a_copies:
        copy.wait_recv()

    for k in range(len(ROWS_UP)):
        dup[k * 8 : k * 8 + 8, :] = unpacked(cor_r[0:8, :], cor_r[8:16, :], k)
    for k in range(len(ROWS_DOWN)):
        ddown[k * 8 : k * 8 + 8, :] = unpacked(cor_r[16:24, :], cor_r[24:32, :], k)

    far_row = gx * 8 + jnp.where(row < 4, row + 8, row - 8)
    far_lane = gy * 128 + jnp.where(lane < 64, lane + 128, lane - 128)
    row_in = (far_row >= 0) & (far_row < n_gx * 8)
    lane_in = (far_lane >= 0) & (far_lane < n_gy * 128)
    inside = [[None, lane_in], [row_in, row_in & lane_in]]
    where_up = {key: k for k, key in enumerate(ROWS_UP)}
    where_down = {key: k for k, key in enumerate(ROWS_DOWN)}

    def border_rows(up, down, c, z):
        o = z - Z0

        def get(ref, k):
            return wide(ref[k * 8 + o : k * 8 + o + 1, :])

        up0, down0 = get(up, where_up[(c, 0)]), get(down, where_down[(c, 7)])
        out = jnp.where(row < 4, up0, down0)
        if (c, 1) in where_up:
            out = jnp.where(row == 1, get(up, where_up[(c, 1)]), out)
        if (c, 6) in where_down:
            out = jnp.where(row == 6, get(down, where_down[(c, 6)]), out)
        return out

    def masked(q, other=0.0):
        return [
            [q[r][n] if inside[r][n] is None else jnp.where(inside[r][n], q[r][n], other) for n in range(2)]
            for r in range(2)
        ]

    def extended(c, z):
        k = TILES_Y.index((c, z))
        q = [
            [own[k * 8 : k * 8 + 8, :], unpacked(col_r[0:8, :], col_r[8:16, :], k)],
            [border_rows(up_r, down_r, c, z), border_rows(dup, ddown, c, z)],
        ]
        return masked(q, 1.0 if c == 6 else 0.0)

    def combine(fn, *qs):
        return [[fn(*[q[r][n] for q in qs]) for n in range(2)] for r in range(2)]

    def turn_x(q, shift, edge):
        out = [[None, None], [None, None]]
        for n in range(2):
            first, second = pltpu.roll(q[0][n], shift, 0), pltpu.roll(q[1][n], shift, 0)
            out[0][n] = jnp.where(row == edge, second, first)
            out[1][n] = jnp.where(row == edge, first, second)
        return out

    def turn_y(q, shift, edge):
        out = []
        for r in range(2):
            first, second = pltpu.roll(q[r][0], shift, 1), pltpu.roll(q[r][1], shift, 1)
            out.append([jnp.where(lane == edge, second, first), jnp.where(lane == edge, first, second)])
        return out

    def ahead_x(q):
        return combine(jnp.subtract, turn_x(q, 7, 7), q)

    def ahead_y(q):
        return combine(jnp.subtract, turn_y(q, 127, 127), q)

    def behind_x(q):
        return combine(jnp.subtract, q, turn_x(q, 1, 0))

    def behind_y(q):
        return combine(jnp.subtract, q, turn_y(q, 1, 0))

    def half(h, one, two):
        return masked(combine(lambda h, p, q: h - TIME_STEP * (p - q), h, one, two))

    def full(e, us, one, two):
        return masked(combine(lambda e, us, p, q: e + us * (p - q), e, us, one, two))

    def minus(p, q):
        return combine(jnp.subtract, p, q)

    def magnetic(e, h, zs):
        for z in zs:
            ex, ey, ez = (e[(c, z)] for c in range(3))
            h[(3, z)] = half(h[(3, z)], ahead_y(ez), minus(e[(1, z + 1)], ey))
            h[(4, z)] = half(h[(4, z)], minus(e[(0, z + 1)], ex), ahead_x(ez))
            h[(5, z)] = half(h[(5, z)], ahead_x(ey), ahead_y(ex))

    e = {(c, z): extended(c, z) for c, z in TILES_Y if c < 3}
    h = {(c, z): extended(c, z) for c, z in TILES_Y if 3 <= c < 6}
    us = {z: combine(lambda p: 0.5 / p, extended(6, z)) for c, z in TILES_Y if c == 6}
    magnetic(e, h, range(Z0, Z0 + 4))
    h1 = [h[(3, ZM)][0][0], h[(4, ZM)][0][0]]
    for z in range(Z0 + 1, Z0 + 4):
        hx, hy, hz = (h[(c, z)] for c in (3, 4, 5))
        e[(0, z)] = full(e[(0, z)], us[z], behind_y(hz), minus(hy, h[(4, z - 1)]))
        e[(1, z)] = full(e[(1, z)], us[z], minus(hx, h[(3, z - 1)]), behind_x(hz))
        e[(2, z)] = full(e[(2, z)], us[z], behind_x(hy), behind_y(hx))
    e1 = [e[(0, ZM)][0][0], e[(1, ZM)][0][0]]
    magnetic(e, h, range(Z0 + 1, Z0 + 3))
    h2 = [h[(3, ZM)][0][0], h[(4, ZM)][0][0]]
    hz = h[(5, ZM)]
    us_m = us[ZM][0][0]
    e2 = [
        e1[0] + us_m * (behind_y(hz)[0][0] - (h2[1] - h[(4, ZM - 1)][0][0])),
        e1[1] + us_m * ((h2[0] - h[(3, ZM - 1)][0][0]) - behind_x(hz)[0][0]),
    ]
    for part_of in range(2):
        first, second = weights_at(0.5)[part_of], weights_at(1.5)[part_of]
        hx, hy = (first * h1[n] + second * h2[n] for n in range(2))
        first, second = weights_at(1)[part_of], weights_at(2)[part_of]
        ex, ey = (first * e1[n] + second * e2[n] for n in range(2))
        for n, value in enumerate((-hy, hx, ey, -ex)):
            gath[0, (part_of * 4 + n) * 8 : (part_of * 4 + n) * 8 + 8, :] = value

    base_g = base + 8
    g_copies = [send(gath.at[0], gath.at[d], base_g + d - 1, zh_peer(d)) for d in range(1, n_zh)]

    for copy in load_rest:
        copy.wait()
    n_w = n_xi * 2 * n_gy
    n_k = n_zh * 16
    wrow = iota((n_w, 128), 0)
    wlane = iota((n_w, 128), 1)
    u = zh * (n_xi * n_gy) + (wrow // (2 * n_gy)) * n_gy + wrow % n_gy
    imag_out = (wrow // n_gy) % 2
    back = wlane // 16
    imag_in = (wlane // 8) % 2
    x = (((zh - back + n_zh) % n_zh) * n_xi + xi) * 8 + wlane % 8
    n_u = n_gx * n_gy
    weights = cos_turns((2 * u + 1 - n_u) * x * (4096 // (16 * n_u)) + 1024 * (imag_out - imag_in))
    hits = jnp.zeros((n_w, 128), F32)
    for d in range(n_zh):
        t = tile_of(d)
        same = (lists_ref[d, pl.ds(t % 8, 1), :] == u[:, : lists_ref.shape[2]]).astype(F32)
        count = jnp.sum(same, axis=1, keepdims=True) * mask_ref[t].astype(F32)
        hits = jnp.where(back == d, count, hits)
    wtab[...] = weights * hits

    def v_rows(b, carry):
        y = b * 32 + iota((32, 512), 0)
        v = iota((32, 512), 1)
        vtab[pl.ds(pl.multiple_of(b * 32, 32), 32), :] = cos_turns(
            (2 * (v & 255) - 255) * y - 1024 * (v >> 8)
        )
        return carry

    lax.fori_loop(0, 4, v_rows, 0)
    d = iota((n_gy, 512), 0)
    v = iota((n_gy, 512), 1)
    tws[...] = cos_turns((2 * (v & 255) - 255) * (((gy - d + n_gy) % n_gy) * 128) - 1024 * (v >> 8))

    electric_step(0, 0)
    magnetic_half(0, 2)

    for copy in g_copies:
        copy.wait_recv()
    table = wtab[:, 0:n_k]
    blk = 8 * n_gy
    for c in range(4):
        planes = jnp.concatenate(
            [gath[d, (4 * r + c) * 8 : (4 * r + c) * 8 + 8, :] for d in range(n_zh) for r in range(2)], axis=0
        )
        out = jnp.dot(table, planes, preferred_element_type=F32, precision=HIGHEST)
        for q in range(n_xi):
            for r in range(2):
                part[q * blk + r * 4 * n_gy + c * n_gy : q * blk + r * 4 * n_gy + (c + 1) * n_gy, :] = out[
                    (q * 2 + r) * n_gy : (q * 2 + r + 1) * n_gy, :
                ]
    base_r = base_g + n_zh - 1
    r_copies = []
    for d in range(1, n_xi):
        to = (xi + d) % n_xi
        r_copies.append(
            send(
                part.at[pl.ds(pl.multiple_of(to * blk, blk), blk)], part_r.at[d - 1], base_r + d - 1, xi_peer(d)
            )
        )

    electric_step(1, 1)
    magnetic_half(1, 3)

    for copy in r_copies:
        copy.wait_recv()
    acc = part[pl.ds(pl.multiple_of(xi * blk, blk), blk), :]
    for d in range(1, n_xi):
        acc = acc + part_r[d - 1]
    total[...] = acc
    for j in range(n_gy):
        rows_s[j] = total[pl.ds(j, 8, stride=n_gy), :]
    rows_r[0] = rows_s[gy]
    base_a = base_r + n_xi - 1
    last_copies = []
    for d in range(1, n_gy):
        to = (gy + d) % n_gy
        last_copies.append(
            send(rows_s.at[to], rows_r.at[d], base_a + d - 1, {"gx": gx, "gy": to})
        )

    last_step()

    for copy in last_copies:
        copy.wait_recv()
    turned = jnp.dot(
        rows_r[...].reshape(n_gy * 8, 128), vtab[...], preferred_element_type=F32, precision=HIGHEST
    )
    sign = jnp.where(iota((8, 256), 0) < 4, 1.0, -1.0)
    out = jnp.zeros((8, 256), F32)
    for d in range(n_gy):
        rows = turned[d * 8 : d * 8 + 8, :]
        value = rows[:, :256] + sign * pltpu.roll(rows[:, 256:], 4, 0)
        out = out + tws[d : d + 1, :256] * value + tws[d : d + 1, 256:] * (sign * pltpu.roll(value, 4, 0))
    far_ref[...] = out * (1.0 / math.sqrt(CX * CY))

    for copy in started:
        copy.wait_send()


def write_out(*refs):
    n = len(refs) // 2
    sems = refs[-1]
    copies = [pltpu.make_async_copy(refs[i], refs[n + i], sems.at[i]) for i in range(n)]
    for copy in copies:
        copy.start()
    for copy in copies:
        copy.wait()


def solution(mesh):
    n_gx, n_gy = mesh.shape["gx"], mesh.shape["gy"]
    n_xi = 4 if n_gx == 16 else n_gx
    dims = (n_gx // n_xi, n_xi, n_gy)
    n_zh = dims[0]
    n_sem = 24 + 8 + (n_zh - 1) + (n_xi - 1) + (n_gy - 1)
    vmem = pl.BlockSpec(memory_space=pltpu.VMEM)
    hbm = pl.BlockSpec(memory_space=pltpu.HBM)
    blk = 8 * n_gy

    def buffer(*shape):
        return pltpu.VMEM(shape, F32)

    def shards(fields, adjoint, permittivity, lists, mask):
        shapes = (
            jax.ShapeDtypeStruct((6 * ROWS, 128), F32),
            jax.ShapeDtypeStruct((6 * ROWS, 128), F32),
            jax.ShapeDtypeStruct((ROWS, 128), F32),
            jax.ShapeDtypeStruct((8, 256), F32),
        )
        made = pl.pallas_call(
            functools.partial(kernel, dims),
            out_shape=tuple(pltpu.VMEM(shape.shape, F32) for shape in shapes),
            in_specs=[hbm] * 5,
            out_specs=(vmem,) * 4,
            scratch_shapes=[
                buffer(ROWS, 128),
                pltpu.VMEM((n_zh, 8, lists.shape[1]), jnp.int32),
                pltpu.SMEM(mask.shape, jnp.int32),
                buffer(ROWS, 128),
                buffer(8 * len(TILES_Y), 128),
                buffer(4, 2 * NZ, 128), buffer(4, 2 * NZ, 128), buffer(4, 2 * NZ, 128), buffer(4, 2 * NZ, 128),
                buffer(4, 16, 128), buffer(4, 16, 128), buffer(4, 16, 128),
                buffer(4, 8, 128), buffer(4, 8, 128), buffer(4, 8, 128), buffer(4, 8, 128),
                buffer(4, 2 * NZ, 128),
                buffer(72, 128), buffer(96, 128), buffer(16, 128), buffer(32, 128),
                buffer(72, 128), buffer(96, 128), buffer(16, 128), buffer(32, 128),
                buffer(72, 128), buffer(96, 128),
                buffer(n_zh, 64, 128), buffer(n_xi * 2 * n_gy, 128), buffer(128, 512), buffer(n_gy, 512),
                buffer(n_xi * blk, 128), buffer(max(n_xi - 1, 1), blk, 128), buffer(blk, 128),
                buffer(n_gy, 8, 128), buffer(n_gy, 8, 128),
                pltpu.SemaphoreType.DMA((4 + n_zh,)),
                pltpu.SemaphoreType.DMA((n_sem,)),
                pltpu.SemaphoreType.DMA((n_sem,)),
            ],
            compiler_params=pltpu.CompilerParams(
                collective_id=0, has_side_effects=True, vmem_limit_bytes=40 * 1024 * 1024
            ),
        )(
            *[
                pltpu.with_memory_space_constraint(value, pltpu.HBM)
                for value in (
                    fields.reshape(6 * ROWS, 128),
                    adjoint.reshape(6 * ROWS, 128),
                    permittivity.reshape(ROWS, 128),
                    lists,
                    mask,
                )
            ]
        )
        out = pl.pallas_call(
            write_out,
            out_shape=shapes,
            in_specs=[pl.BlockSpec(memory_space=pl.ANY)] * 4,
            out_specs=(pl.BlockSpec(memory_space=pl.ANY),) * 4,
            scratch_shapes=[pltpu.SemaphoreType.DMA((4,))],
            compiler_params=pltpu.CompilerParams(vmem_limit_bytes=1024 * 1024),
        )(*made)
        return (
            out[0].reshape(fields.shape),
            out[1].reshape(fields.shape),
            out[2].reshape(permittivity.shape),
            out[3].reshape(1, 8, 256),
        )

    in_specs = (P(None, None, "gx", "gy"), P(None, None, "gx", "gy"), P(None, "gx", "gy"), P(), P())
    out_specs = (
        P(None, None, "gx", "gy"),
        P(None, None, "gx", "gy"),
        P(None, "gx", "gy"),
        P(("gx", "gy"), None, None),
    )
    return jax.shard_map(shards, mesh=mesh, in_specs=in_specs, out_specs=out_specs, check_vma=False)
```

```python
import functools
import math

import jax
import jax.numpy as jnp
from jax import lax
from jax.experimental import pallas as pl
from jax.experimental.pallas import tpu as pltpu
from jax.sharding import PartitionSpec as P

NZ, CX, CY = 48, 8, 128
ROWS = NZ * CX
ZM = 36
Z0 = ZM - 2
TIME_STEP = 0.5
PHASE_STEP = 0.3
OMEGA = PHASE_STEP / TIME_STEP
MESH = pl.DeviceIdType.MESH
F32 = jnp.float32
ZB = 24
NB = NZ // ZB

ROWS_UP = [((0, 0), (6, 0)), ((1, 0),), ((2, 0),), ((3, 0), (4, 0)), ((5, 0), (1, 1)), ((2, 1),)]
ROWS_DOWN = [
    ((0, 7), (6, 7)), ((1, 7),), ((2, 7),), ((3, 7), (4, 7)), ((5, 7), (4, 6)), ((0, 6),), ((1, 6), (2, 6)), ((5, 6),)
]
N_UP, N_DOWN = len(ROWS_UP), len(ROWS_DOWN)
TILES_Y = (
    [(c, z) for c in range(3) for z in range(Z0, Z0 + 5)]
    + [(c, z) for c in range(3, 6) for z in range(Z0, Z0 + 4)]
    + [(6, z) for z in range(Z0 + 1, Z0 + 4)]
)


def weights_at(moment):
    theta = PHASE_STEP * moment
    return (math.cos(theta) * TIME_STEP, -math.sin(theta) * TIME_STEP)


def cos_turns(m):
    m = m + 512
    quarter = (m >> 10) & 3
    angle = ((m & 1023) - 512).astype(F32) * (2.0 * math.pi / 4096)
    a2 = angle * angle
    cosine = 1.0 + a2 * (-0.5 + a2 * (1 / 24 + a2 * (-1 / 720 + a2 * (1 / 40320))))
    sine = angle * (1.0 + a2 * (-1 / 6 + a2 * (1 / 120 + a2 * (-1 / 5040 + a2 * (1 / 362880)))))
    value = jnp.where((quarter & 1) == 1, sine, cosine)
    return jnp.where(((quarter + 1) & 2) == 2, -value, value)


def halves(value):
    high = value.astype(jnp.bfloat16)
    return high, (value - high.astype(F32)).astype(jnp.bfloat16)


def product(left, right):
    return (
        jnp.dot(left[0], right[1], preferred_element_type=F32)
        + jnp.dot(left[1], right[0], preferred_element_type=F32)
    ) + jnp.dot(left[0], right[0], preferred_element_type=F32)


def iota(shape, axis):
    return lax.broadcasted_iota(jnp.int32, shape, axis)


def wide(row):
    return jnp.broadcast_to(row, (8, 128))


def kernel(
    dims,
    f_hbm, a_hbm, eps_hbm, lists_hbm, mask_hbm,
    fo_ref, ao_ref, sens_ref, far_ref,
    eps_ref, lists_ref, mask_ref, scale, slab, mixed,
    es, er, hs, hr, ys, yr_up, yr_down, cxs, cxr, cys, cyr, hrow,
    up_s, down_s, col_s, cor_s, up_r, down_r, col_r, cor_r, dup, ddown,
    gath, wtab, vtab, tws, part, part_r, total, rows_s, rows_r,
    load_sem, send_sem, recv_sem,
):
    n_zh, n_xi, n_gy = dims
    n_gx = n_zh * n_xi
    gx = lax.axis_index("gx")
    gy = lax.axis_index("gy")
    zh = gx // n_xi
    xi = gx % n_xi

    def dev(dx, dy):
        return {"gx": (gx + (dx + n_gx)) % n_gx, "gy": (gy + (dy + n_gy)) % n_gy}

    def zh_peer(d):
        return {"gx": ((zh + d) % n_zh) * n_xi + xi, "gy": gy}

    def xi_peer(d):
        return {"gx": zh * n_xi + (xi + d) % n_xi, "gy": gy}

    def load(src, dst, slot):
        copy = pltpu.make_async_copy(src, dst, load_sem.at[slot])
        copy.start()
        return copy

    def tile_of(d):
        return (((zh - d + n_zh) % n_zh) * n_xi + xi) * n_gy + gy

    load_slab = [
        load(f_hbm.at[pl.ds(c * ROWS + Z0 * 8, 64)], slab.at[pl.ds(c * 64, 64)], 4 + n_zh + c) for c in range(6)
    ]
    load_eps = load(eps_hbm, eps_ref, 1)
    load_f = load(f_hbm, fo_ref, 0)
    load_a = load(a_hbm, ao_ref, 2)
    load_rest = [load(mask_hbm, mask_ref, 3)]
    for d in range(n_zh):
        first = pl.multiple_of(tile_of(d) // 8 * 8, 8)
        load_rest.append(load(lists_hbm.at[pl.ds(first, 8)], lists_ref.at[d], 4 + d))

    barrier = pltpu.get_barrier_semaphore()
    peers = [dev(dx, dy) for dx in (-1, 1) for dy in (-1, 0, 1)]
    peers += [zh_peer(d) for d in range(1, n_zh)] + [xi_peer(d) for d in range(1, n_xi)]
    for peer in peers:
        pl.semaphore_signal(barrier, inc=1, device_id=peer, device_id_type=MESH)

    def greet(d, carry):
        pl.semaphore_signal(
            barrier, inc=1, device_id={"gx": gx, "gy": (gy + d) % n_gy}, device_id_type=MESH
        )
        return carry

    lax.fori_loop(1, n_gy, greet, 0)

    started = []

    def send(src, dst, slot, peer):
        copy = pltpu.make_async_remote_copy(
            src_ref=src, dst_ref=dst, send_sem=send_sem.at[slot], recv_sem=recv_sem.at[slot],
            device_id=peer, device_id_type=MESH,
        )
        copy.start()
        started.append(copy)
        return copy

    row = iota((8, 128), 0)
    lane = iota((8, 128), 1)
    zero = jnp.zeros((8, 128), F32)

    def layer(c, r):
        if c == 6:
            return eps_ref[pl.ds(Z0 * 8 + r, 8, stride=8), :]
        return slab[pl.ds(c * 64 + r, 8, stride=8), :]

    def packed(values, low):
        out = zero
        for k, value in enumerate(values):
            shift = (2 * k if low else 2 * k + 2) % 128
            moved = pltpu.roll(value, shift, 1) if shift else value
            out = jnp.where((lane >> 1) == k, moved, out)
        return out

    def unpacked(low, high, k):
        first = pltpu.roll(low, (128 - 2 * k) % 128, 1) if k else low
        second = pltpu.roll(high, (126 - 2 * k) % 128, 1)
        return jnp.where(lane < 64, first, second)

    for copy in load_slab:
        copy.wait()
    load_eps.wait()
    def layers(keys):
        first = layer(*keys[0])
        if len(keys) == 1:
            return first
        return jnp.where(row < (5 if keys[1][0] == 6 else 4), first, pltpu.roll(layer(*keys[1]), 4, 0))

    ups = [layers(keys) for keys in ROWS_UP]
    downs = [layers(keys) for keys in ROWS_DOWN]
    for k, value in enumerate(ups):
        up_s[k * 8 : k * 8 + 8, :] = value
    for k, value in enumerate(downs):
        down_s[k * 8 : k * 8 + 8, :] = value
    cor_s[0:8, :] = packed(ups, True)
    cor_s[8:16, :] = packed(ups, False)
    cor_s[16:24, :] = packed(downs, True)
    cor_s[24:32, :] = packed(downs, False)
    def tile(c, z):
        if c == 6:
            return eps_ref[z * 8 : z * 8 + 8, :]
        return slab[c * 64 + (z - Z0) * 8 : c * 64 + (z - Z0) * 8 + 8, :]

    tiles_y = [tile(c, z) for c, z in TILES_Y]
    col_s[0:8, :] = packed(tiles_y, True)
    col_s[8:16, :] = packed(tiles_y, False)

    def rows_at(ref, c, r):
        return ref[pl.ds(c * ROWS + r, NZ, stride=8), :]

    def e_rows(ref, k):
        es[k, 0:NZ, :] = rows_at(ref, 1, 0)
        es[k, NZ : 2 * NZ, :] = rows_at(ref, 2, 0)

    states = (fo_ref, ao_ref)
    pending = {}

    def send_e(k):
        pending[k] = [send(es.at[k], er.at[k], k * 6, dev(-1, 0))]

    pl.semaphore_wait(barrier, len(peers) + n_gy - 1)

    base = 24
    a_copies = [
        send(up_s, up_r, base + 0, dev(-1, 0)),
        send(down_s, down_r, base + 1, dev(1, 0)),
        send(col_s.at[0:8], col_r.at[0:8], base + 2, dev(0, -1)),
        send(col_s.at[8:16], col_r.at[8:16], base + 3, dev(0, 1)),
        send(cor_s.at[0:8], cor_r.at[0:8], base + 4, dev(-1, -1)),
        send(cor_s.at[8:16], cor_r.at[8:16], base + 5, dev(-1, 1)),
        send(cor_s.at[16:24], cor_r.at[16:24], base + 6, dev(1, -1)),
        send(cor_s.at[24:32], cor_r.at[24:32], base + 7, dev(1, 1)),
    ]
    load_f.wait()
    e_rows(fo_ref, 0)
    send_e(0)
    load_a.wait()
    e_rows(ao_ref, 1)
    send_e(1)

    def at(ref, c, b, j):
        return ref[pl.ds(pl.multiple_of(c * ROWS + b * (8 * ZB) + j * 8, 8), 8), :]

    def put(ref, c, b, j, value):
        ref[pl.ds(pl.multiple_of(c * ROWS + b * (8 * ZB) + j * 8, 8), 8), :] = value

    def magnetic_half(s, k):
        ref = states[s]

        def body(b, accs):
            ex = [at(ref, 0, b, j) for j in range(ZB + 1)]
            ey = [at(ref, 1, b, j) for j in range(ZB + 1)]
            ez = [at(ref, 2, b, j) for j in range(ZB)]
            old = [[at(ref, c, b, j) for j in range(ZB)] for c in (3, 4, 5)]
            ex[ZB] = jnp.where(b < NB - 1, ex[ZB], 0.0)
            ey[ZB] = jnp.where(b < NB - 1, ey[ZB], 0.0)

            def along_y(value):
                return jnp.where(lane == 127, 0.0, pltpu.roll(value, 127, 1)) - value

            def along_x(value):
                return jnp.where(row == 7, 0.0, pltpu.roll(value, 7, 0)) - value

            news = [zero, zero]
            made = []
            for j in range(ZB):
                hx = old[0][j] - TIME_STEP * (along_y(ez[j]) - (ey[j + 1] - ey[j]))
                hy = old[1][j] - TIME_STEP * ((ex[j + 1] - ex[j]) - along_x(ez[j]))
                hz = old[2][j] - TIME_STEP * (along_x(ey[j]) - along_y(ex[j]))
                made.append((hx, hy, hz))
                for n, (h, e) in enumerate(((hx, ex[j]), (hz, ez[j]))):
                    both = pltpu.roll(jnp.where(lane == 127, h, e), 2 * j + 1, 1)
                    news[n] = jnp.where((lane >> 1) == j, both, news[n])
            for j in range(ZB):
                for n in range(3):
                    put(ref, 3 + n, b, j, made[j][n])
            return tuple(
                jnp.where(lane // (2 * ZB) == b, pltpu.roll(new, b * (2 * ZB), 1), acc)
                for acc, new in zip(accs, news)
            )

        low, high = lax.fori_loop(0, NB, body, (zero, zero))
        ys[k, 0:8, :] = low
        ys[k, 8:16, :] = high
        hs[k, 0:NZ, :] = rows_at(ref, 4, 7)
        hs[k, NZ : 2 * NZ, :] = rows_at(ref, 5, 7)
        corner = zero
        for m in range(NZ // 8):
            piece = ref[pl.ds(m * 64 + 7, 8, stride=8), :]
            corner = jnp.where(lane == m, pltpu.roll(piece, m, 1) if m else piece, corner)
        cxs[k] = corner
        corner = zero
        for m in range(NZ // 8):
            piece = jnp.broadcast_to(es[k, m * 8 : m * 8 + 8, 127:128], (8, 128))
            corner = jnp.where(lane == 16 * m + 2 * row + 1, piece, corner)
        cys[k] = jnp.broadcast_to(jnp.sum(corner, axis=0, keepdims=True), (8, 128))
        pending[k] += [
            send(hs.at[k], hr.at[k], k * 6 + 1, dev(1, 0)),
            send(ys.at[k], yr_up.at[k], k * 6 + 2, dev(0, -1)),
            send(ys.at[k], yr_down.at[k], k * 6 + 3, dev(0, 1)),
            send(cxs.at[k], cxr.at[k], k * 6 + 4, dev(1, -1)),
            send(cys.at[k], cyr.at[k], k * 6 + 5, dev(-1, 1)),
        ]

    has_next_x = jnp.where(gx < n_gx - 1, 1.0, 0.0)
    has_previous_x = jnp.where(gx > 0, 1.0, 0.0)
    has_next_y = jnp.where(gy < n_gy - 1, 1.0, 0.0)
    has_previous_y = jnp.where(gy > 0, 1.0, 0.0)

    def add_rows(ref, c, value):
        ref[pl.ds(c * ROWS + 7, NZ, stride=8), :] = rows_at(ref, c, 7) + value

    def borders(s, k):
        ref = states[s]
        for copy in pending[k]:
            copy.wait_recv()
        add_rows(ref, 4, er[k, NZ : 2 * NZ, :] * (TIME_STEP * has_next_x))
        add_rows(ref, 5, er[k, 0:NZ, :] * (-TIME_STEP * has_next_x))
        hrow[k, 0:NZ, :] = (hr[k, 0:NZ, :] + TIME_STEP * es[k, NZ : 2 * NZ, :]) * has_previous_x
        for m in range(NZ // 8):
            o = m * 8
            side = jnp.where(lane == 127, pltpu.roll(cxr[k], 127 - m, 1), 0.0) * (TIME_STEP * has_next_y)
            hrow[k, NZ + o : NZ + o + 8, :] = (
                hr[k, NZ + o : NZ + o + 8, :] - TIME_STEP * es[k, o : o + 8, :] + side
            ) * has_previous_x
        corner = jnp.where(row == 7, cyr[k], 0.0) * (TIME_STEP * has_next_x)
        even = (lane & 1) == 0
        return [
            jnp.where(
                even,
                pltpu.roll(up_e, 127, 1) * (factor * has_next_y),
                (down_h + factor * own_e - other) * has_previous_y,
            )
            for up_e, down_h, own_e, factor, other in (
                (yr_up[k, 8:16, :], pltpu.roll(yr_down[k, 0:8, :], 1, 1), ys[k, 8:16, :], -TIME_STEP, zero),
                (yr_up[k, 0:8, :], pltpu.roll(yr_down[k, 8:16, :], 1, 1), ys[k, 0:8, :], TIME_STEP, corner),
            )
        ]

    def electric_block(s, k, sides, b):
        ref = states[s]
        moved = [pltpu.roll(side, 128 - b * (2 * ZB), 1) for side in sides]
        hx, hy, hz = ([at(ref, c, b, j) for j in range(-1 if c < 5 else 0, ZB)] for c in (3, 4, 5))
        hx[0] = jnp.where(b > 0, hx[0], 0.0)
        hy[0] = jnp.where(b > 0, hy[0], 0.0)
        old = [[at(ref, c, b, j) for c in range(3)] for j in range(ZB)]
        us = [at(scale, 0, b, j) for j in range(ZB)]
        behind_hx, behind_hz = [], []
        for j in range(ZB):
            for n, values, o, out in ((0, hx, j + 1, behind_hx), (1, hz, j, behind_hz)):
                side = pltpu.roll(moved[n], 127 - 2 * j, 1)
                values[o] = values[o] + jnp.where(lane == 127, side, 0.0)
                out.append(values[o] - jnp.where(lane == 0, side, pltpu.roll(values[o], 1, 1)))
        new = []
        for j in range(ZB):

            def along_x(value, n, j=j):
                side = wide(hrow[k, pl.ds(n * NZ + b * ZB + j, 1), :])
                return value - jnp.where(row == 0, side, pltpu.roll(value, 1, 0))

            new.append(
                (
                    old[j][0] + us[j] * (behind_hz[j] - (hy[j + 1] - hy[j])),
                    old[j][1] + us[j] * ((hx[j + 1] - hx[j]) - along_x(hz[j], 1)),
                    old[j][2] + us[j] * (along_x(hy[j + 1], 0) - behind_hx[j]),
                )
            )
        for j in range(ZB):
            for n in range(3):
                put(ref, n, b, j, new[j][n])
            put(ref, 3, b, j, hx[j + 1])
            put(ref, 5, b, j, hz[j])
        return old, new

    def electric_step(s, k):
        sides = borders(s, k)

        def body(b, carry):
            electric_block(s, k, sides, b)
            return carry

        lax.fori_loop(0, NB, body, 0)
        e_rows(states[s], k + 2)
        send_e(k + 2)

    (a1, b1), (a2, b2) = weights_at(1), weights_at(2)
    k11, k12, k22 = (OMEGA**2 * k for k in (a1 * a1 - b1 * b1, a1 * a2 - b1 * b2, a2 * a2 - b2 * b2))

    def last_forward():
        sides = borders(0, 2)

        def body(b, carry):
            old, new = electric_block(0, 2, sides, b)
            for j in range(ZB):
                for n in range(3):
                    put(mixed, n, b, j, k11 * old[j][n] + k12 * new[j][n])
                    put(mixed, 3 + n, b, j, k12 * old[j][n] + k22 * new[j][n])
            return carry

        lax.fori_loop(0, NB, body, 0)

    def last_adjoint():
        sides = borders(1, 3)

        def body(b, carry):
            old, new = electric_block(1, 3, sides, b)
            for j in range(ZB):
                terms = [old[j][n] * at(mixed, n, b, j) + new[j][n] * at(mixed, 3 + n, b, j) for n in range(3)]
                put(sens_ref, 0, b, j, terms[0] + terms[1] + terms[2])
            return carry

        lax.fori_loop(0, NB, body, 0)

    for s in range(2):
        magnetic_half(s, s)

    def scales(b, carry):
        rows = pl.ds(pl.multiple_of(b * 192, 192), 192)
        scale[rows, :] = 0.5 / eps_ref[rows, :]
        return carry

    lax.fori_loop(0, ROWS // 192, scales, 0)

    for copy in a_copies:
        copy.wait_recv()

    for k in range(len(ROWS_UP)):
        dup[k * 8 : k * 8 + 8, :] = unpacked(cor_r[0:8, :], cor_r[8:16, :], k)
    for k in range(len(ROWS_DOWN)):
        ddown[k * 8 : k * 8 + 8, :] = unpacked(cor_r[16:24, :], cor_r[24:32, :], k)

    far_row = gx * 8 + jnp.where(row < 4, row + 8, row - 8)
    far_lane = gy * 128 + jnp.where(lane < 64, lane + 128, lane - 128)
    row_in = (far_row >= 0) & (far_row < n_gx * 8)
    lane_in = (far_lane >= 0) & (far_lane < n_gy * 128)
    inside = [[None, lane_in], [row_in, row_in & lane_in]]
    where_up, where_down = (
        {key: 8 * k + 4 * n for k, keys in enumerate(table) for n, key in enumerate(keys)}
        for table in (ROWS_UP, ROWS_DOWN)
    )

    def border_rows(up, down, c, z):
        o = z - Z0

        def get(ref, start):
            at_z = start + (o if start % 8 + o < 8 else 0)
            return wide(ref[at_z : at_z + 1, :])

        up0, down0 = get(up, where_up[(c, 0)]), get(down, where_down[(c, 7)])
        out = jnp.where(row < 4, up0, down0)
        if (c, 1) in where_up:
            out = jnp.where(row == 1, get(up, where_up[(c, 1)]), out)
        if (c, 6) in where_down:
            out = jnp.where(row == 6, get(down, where_down[(c, 6)]), out)
        return out

    def masked(q, other=0.0):
        return [
            [q[r][n] if inside[r][n] is None else jnp.where(inside[r][n], q[r][n], other) for n in range(2)]
            for r in range(2)
        ]

    def extended(c, z):
        k = TILES_Y.index((c, z))
        q = [
            [tile(c, z), unpacked(col_r[0:8, :], col_r[8:16, :], k)],
            [border_rows(up_r, down_r, c, z), border_rows(dup, ddown, c, z)],
        ]
        return masked(q, 1.0 if c == 6 else 0.0)

    def combine(fn, *qs):
        return [[fn(*[q[r][n] for q in qs]) for n in range(2)] for r in range(2)]

    def turn_x(q, shift, edge):
        out = [[None, None], [None, None]]
        for n in range(2):
            first, second = pltpu.roll(q[0][n], shift, 0), pltpu.roll(q[1][n], shift, 0)
            out[0][n] = jnp.where(row == edge, second, first)
            out[1][n] = jnp.where(row == edge, first, second)
        return out

    def turn_y(q, shift, edge):
        out = []
        for r in range(2):
            first, second = pltpu.roll(q[r][0], shift, 1), pltpu.roll(q[r][1], shift, 1)
            out.append([jnp.where(lane == edge, second, first), jnp.where(lane == edge, first, second)])
        return out

    def ahead_x(q):
        return combine(jnp.subtract, turn_x(q, 7, 7), q)

    def ahead_y(q):
        return combine(jnp.subtract, turn_y(q, 127, 127), q)

    def behind_x(q):
        return combine(jnp.subtract, q, turn_x(q, 1, 0))

    def behind_y(q):
        return combine(jnp.subtract, q, turn_y(q, 1, 0))

    def half(h, one, two):
        return masked(combine(lambda h, p, q: h - TIME_STEP * (p - q), h, one, two))

    def full(e, us, one, two):
        return masked(combine(lambda e, us, p, q: e + us * (p - q), e, us, one, two))

    def minus(p, q):
        return combine(jnp.subtract, p, q)

    def magnetic(e, h, zs):
        for z in zs:
            ex, ey, ez = (e[(c, z)] for c in range(3))
            h[(3, z)] = half(h[(3, z)], ahead_y(ez), minus(e[(1, z + 1)], ey))
            h[(4, z)] = half(h[(4, z)], minus(e[(0, z + 1)], ex), ahead_x(ez))
            h[(5, z)] = half(h[(5, z)], ahead_x(ey), ahead_y(ex))

    e = {(c, z): extended(c, z) for c, z in TILES_Y if c < 3}
    h = {(c, z): extended(c, z) for c, z in TILES_Y if 3 <= c < 6}
    us = {z: combine(lambda p: 0.5 / p, extended(6, z)) for c, z in TILES_Y if c == 6}
    magnetic(e, h, range(Z0, Z0 + 4))
    h1 = [h[(3, ZM)][0][0], h[(4, ZM)][0][0]]
    for z in range(Z0 + 1, Z0 + 4):
        hx, hy, hz = (h[(c, z)] for c in (3, 4, 5))
        e[(0, z)] = full(e[(0, z)], us[z], behind_y(hz), minus(hy, h[(4, z - 1)]))
        e[(1, z)] = full(e[(1, z)], us[z], minus(hx, h[(3, z - 1)]), behind_x(hz))
        e[(2, z)] = full(e[(2, z)], us[z], behind_x(hy), behind_y(hx))
    e1 = [e[(0, ZM)][0][0], e[(1, ZM)][0][0]]
    magnetic(e, h, range(Z0 + 1, Z0 + 3))
    h2 = [h[(3, ZM)][0][0], h[(4, ZM)][0][0]]
    hz = h[(5, ZM)]
    us_m = us[ZM][0][0]
    e2 = [
        e1[0] + us_m * (behind_y(hz)[0][0] - (h2[1] - h[(4, ZM - 1)][0][0])),
        e1[1] + us_m * ((h2[0] - h[(3, ZM - 1)][0][0]) - behind_x(hz)[0][0]),
    ]
    for part_of in range(2):
        first, second = weights_at(0.5)[part_of], weights_at(1.5)[part_of]
        hx, hy = (first * h1[n] + second * h2[n] for n in range(2))
        first, second = weights_at(1)[part_of], weights_at(2)[part_of]
        ex, ey = (first * e1[n] + second * e2[n] for n in range(2))
        for n, value in enumerate((-hy, hx, ey, -ex)):
            gath[0, (part_of * 4 + n) * 8 : (part_of * 4 + n) * 8 + 8, :] = value

    base_g = base + 8
    g_copies = [send(gath.at[0], gath.at[d], base_g + d - 1, zh_peer(d)) for d in range(1, n_zh)]

    for copy in load_rest:
        copy.wait()
    n_w = n_xi * 2 * n_gy
    n_k = n_zh * 16
    wrow = iota((n_w, 128), 0)
    wlane = iota((n_w, 128), 1)
    u = zh * (n_xi * n_gy) + (wrow // (2 * n_gy)) * n_gy + wrow % n_gy
    imag_out = (wrow // n_gy) % 2
    back = wlane // 16
    imag_in = (wlane // 8) % 2
    x = (((zh - back + n_zh) % n_zh) * n_xi + xi) * 8 + wlane % 8
    n_u = n_gx * n_gy
    weights = cos_turns((2 * u + 1 - n_u) * x * (4096 // (16 * n_u)) + 1024 * (imag_out - imag_in))
    hits = jnp.zeros((n_w, 128), F32)
    for d in range(n_zh):
        t = tile_of(d)
        same = (lists_ref[d, pl.ds(t % 8, 1), :] == u[:, : lists_ref.shape[2]]).astype(F32)
        count = jnp.sum(same, axis=1, keepdims=True) * mask_ref[t].astype(F32)
        hits = jnp.where(back == d, count, hits)
    wtab[0], wtab[1] = halves(weights * hits)

    def v_rows(b, carry):
        y = b * 32 + iota((32, 512), 0)
        v = iota((32, 512), 1)
        rows = pl.ds(pl.multiple_of(b * 32, 32), 32)
        vtab[0, rows, :], vtab[1, rows, :] = halves(cos_turns((2 * (v & 255) - 255) * y - 1024 * (v >> 8)))
        return carry

    lax.fori_loop(0, 4, v_rows, 0)
    d = iota((n_gy, 512), 0)
    v = iota((n_gy, 512), 1)
    tws[...] = cos_turns((2 * (v & 255) - 255) * (((gy - d + n_gy) % n_gy) * 128) - 1024 * (v >> 8))

    electric_step(0, 0)
    magnetic_half(0, 2)

    for copy in g_copies:
        copy.wait_recv()
    table = (wtab[0][:, 0:n_k], wtab[1][:, 0:n_k])
    blk = 8 * n_gy
    for c in range(4):
        planes = jnp.concatenate(
            [gath[d, (4 * r + c) * 8 : (4 * r + c) * 8 + 8, :] for d in range(n_zh) for r in range(2)], axis=0
        )
        out = product(table, halves(planes))
        for q in range(n_xi):
            for r in range(2):
                part[q * blk + r * 4 * n_gy + c * n_gy : q * blk + r * 4 * n_gy + (c + 1) * n_gy, :] = out[
                    (q * 2 + r) * n_gy : (q * 2 + r + 1) * n_gy, :
                ]
    base_r = base_g + n_zh - 1
    r_copies = []
    for d in range(1, n_xi):
        to = (xi + d) % n_xi
        r_copies.append(
            send(
                part.at[pl.ds(pl.multiple_of(to * blk, blk), blk)], part_r.at[d - 1], base_r + d - 1, xi_peer(d)
            )
        )

    electric_step(1, 1)
    magnetic_half(1, 3)

    for copy in r_copies:
        copy.wait_recv()
    acc = part[pl.ds(pl.multiple_of(xi * blk, blk), blk), :]
    for d in range(1, n_xi):
        acc = acc + part_r[d - 1]
    total[...] = acc
    for j in range(n_gy):
        rows_s[j] = total[pl.ds(j, 8, stride=n_gy), :]
    rows_r[0] = rows_s[gy]
    base_a = base_r + n_xi - 1
    last_copies = []
    for d in range(1, n_gy):
        to = (gy + d) % n_gy
        last_copies.append(
            send(rows_s.at[to], rows_r.at[d], base_a + d - 1, {"gx": gx, "gy": to})
        )

    last_forward()
    last_adjoint()

    for copy in last_copies:
        copy.wait_recv()
    turned = product(halves(rows_r[...].reshape(n_gy * 8, 128)), (vtab[0], vtab[1]))
    sign = jnp.where(iota((8, 256), 0) < 4, 1.0, -1.0)
    out = jnp.zeros((8, 256), F32)
    for d in range(n_gy):
        rows = turned[d * 8 : d * 8 + 8, :]
        value = rows[:, :256] + sign * pltpu.roll(rows[:, 256:], 4, 0)
        out = out + tws[d : d + 1, :256] * value + tws[d : d + 1, 256:] * (sign * pltpu.roll(value, 4, 0))
    far_ref[...] = out * (1.0 / math.sqrt(CX * CY))

    for copy in started:
        copy.wait_send()


PIECES = ((0, 4), (1, 4), (2, 1), (3, 1))


def write_out(*refs):
    sems = refs[-1]
    copies = []
    for i, pieces in PIECES:
        rows = refs[i].shape[0] // pieces
        for p in range(pieces):
            part = pl.ds(p * rows, rows)
            copies.append(pltpu.make_async_copy(refs[i].at[part], refs[4 + i].at[part], sems.at[len(copies)]))
    for copy in copies:
        copy.start()
    for copy in copies:
        copy.wait()


def solution(mesh):
    n_gx, n_gy = mesh.shape["gx"], mesh.shape["gy"]
    n_xi = 4 if n_gx == 16 else n_gx
    dims = (n_gx // n_xi, n_xi, n_gy)
    n_zh = dims[0]
    n_sem = 24 + 8 + (n_zh - 1) + (n_xi - 1) + (n_gy - 1)
    vmem = pl.BlockSpec(memory_space=pltpu.VMEM)
    hbm = pl.BlockSpec(memory_space=pltpu.HBM)
    blk = 8 * n_gy

    def buffer(*shape):
        return pltpu.VMEM(shape, F32)

    def shards(fields, adjoint, permittivity, lists, mask):
        shapes = (
            jax.ShapeDtypeStruct((6 * ROWS, 128), F32),
            jax.ShapeDtypeStruct((6 * ROWS, 128), F32),
            jax.ShapeDtypeStruct((ROWS, 128), F32),
            jax.ShapeDtypeStruct((8, 256), F32),
        )
        made = pl.pallas_call(
            functools.partial(kernel, dims),
            out_shape=tuple(pltpu.VMEM(shape.shape, F32) for shape in shapes),
            in_specs=[hbm] * 5,
            out_specs=(vmem,) * 4,
            scratch_shapes=[
                buffer(ROWS, 128),
                pltpu.VMEM((n_zh, 8, lists.shape[1]), jnp.int32),
                pltpu.SMEM(mask.shape, jnp.int32),
                buffer(ROWS, 128),
                buffer(6 * 64, 128), buffer(6 * ROWS, 128),
                buffer(4, 2 * NZ, 128), buffer(4, 2 * NZ, 128), buffer(4, 2 * NZ, 128), buffer(4, 2 * NZ, 128),
                buffer(4, 16, 128), buffer(4, 16, 128), buffer(4, 16, 128),
                buffer(4, 8, 128), buffer(4, 8, 128), buffer(4, 8, 128), buffer(4, 8, 128),
                buffer(4, 2 * NZ, 128),
                buffer(8 * N_UP, 128), buffer(8 * N_DOWN, 128), buffer(16, 128), buffer(32, 128),
                buffer(8 * N_UP, 128), buffer(8 * N_DOWN, 128), buffer(16, 128), buffer(32, 128),
                buffer(8 * N_UP, 128), buffer(8 * N_DOWN, 128),
                buffer(n_zh, 64, 128), pltpu.VMEM((2, n_xi * 2 * n_gy, 128), jnp.bfloat16), pltpu.VMEM((2, 128, 512), jnp.bfloat16), buffer(n_gy, 512),
                buffer(n_xi * blk, 128), buffer(max(n_xi - 1, 1), blk, 128), buffer(blk, 128),
                buffer(n_gy, 8, 128), buffer(n_gy, 8, 128),
                pltpu.SemaphoreType.DMA((4 + n_zh + 6,)),
                pltpu.SemaphoreType.DMA((n_sem,)),
                pltpu.SemaphoreType.DMA((n_sem,)),
            ],
            compiler_params=pltpu.CompilerParams(
                collective_id=0, has_side_effects=True, vmem_limit_bytes=40 * 1024 * 1024
            ),
        )(
            *[
                pltpu.with_memory_space_constraint(value, pltpu.HBM)
                for value in (
                    fields.reshape(6 * ROWS, 128),
                    adjoint.reshape(6 * ROWS, 128),
                    permittivity.reshape(ROWS, 128),
                    lists,
                    mask,
                )
            ]
        )
        out = pl.pallas_call(
            write_out,
            out_shape=shapes,
            in_specs=[pl.BlockSpec(memory_space=pl.ANY)] * 4,
            out_specs=(pl.BlockSpec(memory_space=pl.ANY),) * 4,
            scratch_shapes=[pltpu.SemaphoreType.DMA((10,))],
            compiler_params=pltpu.CompilerParams(vmem_limit_bytes=1024 * 1024),
        )(*made)
        return (
            out[0].reshape(fields.shape),
            out[1].reshape(fields.shape),
            out[2].reshape(permittivity.shape),
            out[3].reshape(1, 8, 256),
        )

    in_specs = (P(None, None, "gx", "gy"), P(None, None, "gx", "gy"), P(None, "gx", "gy"), P(), P())
    out_specs = (
        P(None, None, "gx", "gy"),
        P(None, None, "gx", "gy"),
        P(None, "gx", "gy"),
        P(("gx", "gy"), None, None),
    )
    return jax.shard_map(shards, mesh=mesh, in_specs=in_specs, out_specs=out_specs, check_vma=False)
```

```python
import functools
import math

import jax
import jax.numpy as jnp
from jax import lax
from jax.experimental import pallas as pl
from jax.experimental.pallas import tpu as pltpu
from jax.sharding import PartitionSpec as P

NZ, CX, CY = 48, 8, 128
ROWS = NZ * CX
ZM = 36
Z0 = ZM - 2
TIME_STEP = 0.5
PHASE_STEP = 0.3
OMEGA = PHASE_STEP / TIME_STEP
MESH = pl.DeviceIdType.MESH
F32 = jnp.float32
ZB = 24
NB = NZ // ZB

ROWS_UP = [((0, 0), (6, 0)), ((1, 0),), ((2, 0),), ((3, 0), (4, 0)), ((5, 0), (1, 1)), ((2, 1),)]
ROWS_DOWN = [
    ((0, 7), (6, 7)), ((1, 7),), ((2, 7),), ((3, 7), (4, 7)), ((5, 7), (4, 6)), ((0, 6),), ((1, 6), (2, 6)), ((5, 6),)
]
N_UP, N_DOWN = len(ROWS_UP), len(ROWS_DOWN)
TILES_Y = (
    [(c, z) for c in range(3) for z in range(Z0, Z0 + 5)]
    + [(c, z) for c in range(3, 6) for z in range(Z0, Z0 + 4)]
    + [(6, z) for z in range(Z0 + 1, Z0 + 4)]
)


def weights_at(moment):
    theta = PHASE_STEP * moment
    return (math.cos(theta) * TIME_STEP, -math.sin(theta) * TIME_STEP)


def cos_turns(m):
    m = m + 512
    quarter = (m >> 10) & 3
    angle = ((m & 1023) - 512).astype(F32) * (2.0 * math.pi / 4096)
    a2 = angle * angle
    cosine = 1.0 + a2 * (-0.5 + a2 * (1 / 24 + a2 * (-1 / 720 + a2 * (1 / 40320))))
    sine = angle * (1.0 + a2 * (-1 / 6 + a2 * (1 / 120 + a2 * (-1 / 5040 + a2 * (1 / 362880)))))
    value = jnp.where((quarter & 1) == 1, sine, cosine)
    return jnp.where(((quarter + 1) & 2) == 2, -value, value)


def halves(value):
    high = value.astype(jnp.bfloat16)
    return high, (value - high.astype(F32)).astype(jnp.bfloat16)


def product(left, right):
    return (
        jnp.dot(left[0], right[1], preferred_element_type=F32)
        + jnp.dot(left[1], right[0], preferred_element_type=F32)
    ) + jnp.dot(left[0], right[0], preferred_element_type=F32)


def iota(shape, axis):
    return lax.broadcasted_iota(jnp.int32, shape, axis)


def wide(row):
    return jnp.broadcast_to(row, (8, 128))


def kernel(
    dims,
    f_hbm, a_hbm, eps_hbm, lists_hbm, mask_hbm,
    fo_ref, ao_ref, sens_ref, far_ref,
    eps_ref, lists_ref, mask_ref, scale, slab, mixed,
    es, er, hs, hr, ys, yr_up, yr_down, cxs, cxr, cys, cyr, hrow,
    up_s, down_s, col_s, cor_s, up_r, down_r, col_r, cor_r, dup, ddown,
    gath, wtab, vtab, tws, part, part_r, total, rows_s, rows_r,
    load_sem, send_sem, recv_sem,
):
    n_zh, n_xi, n_gy = dims
    n_gx = n_zh * n_xi
    gx = lax.axis_index("gx")
    gy = lax.axis_index("gy")
    zh = gx // n_xi
    xi = gx % n_xi

    def dev(dx, dy):
        return {"gx": (gx + (dx + n_gx)) % n_gx, "gy": (gy + (dy + n_gy)) % n_gy}

    def zh_peer(d):
        return {"gx": ((zh + d) % n_zh) * n_xi + xi, "gy": gy}

    def xi_peer(d):
        return {"gx": zh * n_xi + (xi + d) % n_xi, "gy": gy}

    def load(src, dst, slot):
        copy = pltpu.make_async_copy(src, dst, load_sem.at[slot])
        copy.start()
        return copy

    def tile_of(d):
        return (((zh - d + n_zh) % n_zh) * n_xi + xi) * n_gy + gy

    load_slab = [
        load(f_hbm.at[pl.ds(c * ROWS + Z0 * 8, 64)], slab.at[pl.ds(c * 64, 64)], 4 + n_zh + c) for c in range(6)
    ]
    load_eps = load(eps_hbm, eps_ref, 1)
    load_f = load(f_hbm, fo_ref, 0)
    load_a = load(a_hbm, ao_ref, 2)
    load_rest = [load(mask_hbm, mask_ref, 3)]
    for d in range(n_zh):
        first = pl.multiple_of(tile_of(d) // 8 * 8, 8)
        load_rest.append(load(lists_hbm.at[pl.ds(first, 8)], lists_ref.at[d], 4 + d))

    barrier = pltpu.get_barrier_semaphore()
    peers = [dev(dx, dy) for dx in (-1, 1) for dy in (-1, 0, 1)]
    peers += [zh_peer(d) for d in range(1, n_zh)] + [xi_peer(d) for d in range(1, n_xi)]
    for peer in peers:
        pl.semaphore_signal(barrier, inc=1, device_id=peer, device_id_type=MESH)

    def greet(d, carry):
        pl.semaphore_signal(
            barrier, inc=1, device_id={"gx": gx, "gy": (gy + d) % n_gy}, device_id_type=MESH
        )
        return carry

    lax.fori_loop(1, n_gy, greet, 0)

    started = []

    def send(src, dst, slot, peer):
        copy = pltpu.make_async_remote_copy(
            src_ref=src, dst_ref=dst, send_sem=send_sem.at[slot], recv_sem=recv_sem.at[slot],
            device_id=peer, device_id_type=MESH,
        )
        copy.start()
        started.append(copy)
        return copy

    row = iota((8, 128), 0)
    lane = iota((8, 128), 1)
    zero = jnp.zeros((8, 128), F32)

    def layer(c, r):
        if c == 6:
            return eps_ref[pl.ds(Z0 * 8 + r, 8, stride=8), :]
        return slab[pl.ds(c * 64 + r, 8, stride=8), :]

    def packed(values, low):
        out = zero
        for k, value in enumerate(values):
            shift = (2 * k if low else 2 * k + 2) % 128
            moved = pltpu.roll(value, shift, 1) if shift else value
            out = jnp.where((lane >> 1) == k, moved, out)
        return out

    def unpacked(low, high, k):
        first = pltpu.roll(low, (128 - 2 * k) % 128, 1) if k else low
        second = pltpu.roll(high, (126 - 2 * k) % 128, 1)
        return jnp.where(lane < 64, first, second)

    for copy in load_slab:
        copy.wait()
    load_eps.wait()
    def layers(keys):
        first = layer(*keys[0])
        if len(keys) == 1:
            return first
        return jnp.where(row < (5 if keys[1][0] == 6 else 4), first, pltpu.roll(layer(*keys[1]), 4, 0))

    ups = [layers(keys) for keys in ROWS_UP]
    downs = [layers(keys) for keys in ROWS_DOWN]
    for k, value in enumerate(ups):
        up_s[k * 8 : k * 8 + 8, :] = value
    for k, value in enumerate(downs):
        down_s[k * 8 : k * 8 + 8, :] = value
    cor_s[0:8, :] = packed(ups, True)
    cor_s[8:16, :] = packed(ups, False)
    cor_s[16:24, :] = packed(downs, True)
    cor_s[24:32, :] = packed(downs, False)
    def tile(c, z):
        if c == 6:
            return eps_ref[z * 8 : z * 8 + 8, :]
        return slab[c * 64 + (z - Z0) * 8 : c * 64 + (z - Z0) * 8 + 8, :]

    tiles_y = [tile(c, z) for c, z in TILES_Y]
    col_s[0:8, :] = packed(tiles_y, True)
    col_s[8:16, :] = packed(tiles_y, False)

    def rows_at(ref, c, r):
        return ref[pl.ds(c * ROWS + r, NZ, stride=8), :]

    def e_rows(ref, k):
        es[k, 0:NZ, :] = rows_at(ref, 1, 0)
        es[k, NZ : 2 * NZ, :] = rows_at(ref, 2, 0)

    states = (fo_ref, ao_ref)
    pending = {}

    def send_e(k):
        pending[k] = [send(es.at[k], er.at[k], k * 6, dev(-1, 0))]

    pl.semaphore_wait(barrier, len(peers) + n_gy - 1)

    base = 24
    a_copies = [
        send(up_s, up_r, base + 0, dev(-1, 0)),
        send(down_s, down_r, base + 1, dev(1, 0)),
        send(col_s.at[0:8], col_r.at[0:8], base + 2, dev(0, -1)),
        send(col_s.at[8:16], col_r.at[8:16], base + 3, dev(0, 1)),
        send(cor_s.at[0:8], cor_r.at[0:8], base + 4, dev(-1, -1)),
        send(cor_s.at[8:16], cor_r.at[8:16], base + 5, dev(-1, 1)),
        send(cor_s.at[16:24], cor_r.at[16:24], base + 6, dev(1, -1)),
        send(cor_s.at[24:32], cor_r.at[24:32], base + 7, dev(1, 1)),
    ]
    load_f.wait()
    e_rows(fo_ref, 0)
    send_e(0)
    load_a.wait()
    e_rows(ao_ref, 1)
    send_e(1)

    def at(ref, c, b, j):
        return ref[pl.ds(pl.multiple_of(c * ROWS + b * (8 * ZB) + j * 8, 8), 8), :]

    def put(ref, c, b, j, value):
        ref[pl.ds(pl.multiple_of(c * ROWS + b * (8 * ZB) + j * 8, 8), 8), :] = value

    def magnetic_half(s, k):
        ref = states[s]

        def body(b, accs):
            ex = [at(ref, 0, b, j) for j in range(ZB + 1)]
            ey = [at(ref, 1, b, j) for j in range(ZB + 1)]
            ez = [at(ref, 2, b, j) for j in range(ZB)]
            old = [[at(ref, c, b, j) for j in range(ZB)] for c in (3, 4, 5)]
            ex[ZB] = jnp.where(b < NB - 1, ex[ZB], 0.0)
            ey[ZB] = jnp.where(b < NB - 1, ey[ZB], 0.0)

            def along_y(value):
                return jnp.where(lane == 127, 0.0, pltpu.roll(value, 127, 1)) - value

            def along_x(value):
                return jnp.where(row == 7, 0.0, pltpu.roll(value, 7, 0)) - value

            news = [zero, zero]
            made = []
            for j in range(ZB):
                hx = old[0][j] - TIME_STEP * (along_y(ez[j]) - (ey[j + 1] - ey[j]))
                hy = old[1][j] - TIME_STEP * ((ex[j + 1] - ex[j]) - along_x(ez[j]))
                hz = old[2][j] - TIME_STEP * (along_x(ey[j]) - along_y(ex[j]))
                made.append((hx, hy, hz))
                for n, (h, e) in enumerate(((hx, ex[j]), (hz, ez[j]))):
                    both = pltpu.roll(jnp.where(lane == 127, h, e), 2 * j + 1, 1)
                    news[n] = jnp.where((lane >> 1) == j, both, news[n])
            for j in range(ZB):
                for n in range(3):
                    put(ref, 3 + n, b, j, made[j][n])
            return tuple(
                jnp.where(lane // (2 * ZB) == b, pltpu.roll(new, b * (2 * ZB), 1), acc)
                for acc, new in zip(accs, news)
            )

        low, high = lax.fori_loop(0, NB, body, (zero, zero))
        ys[k, 0:8, :] = low
        ys[k, 8:16, :] = high
        hs[k, 0:NZ, :] = rows_at(ref, 4, 7)
        hs[k, NZ : 2 * NZ, :] = rows_at(ref, 5, 7)
        corner = zero
        for m in range(NZ // 8):
            piece = ref[pl.ds(m * 64 + 7, 8, stride=8), :]
            corner = jnp.where(lane == m, pltpu.roll(piece, m, 1) if m else piece, corner)
        cxs[k] = corner
        corner = zero
        for m in range(NZ // 8):
            piece = jnp.broadcast_to(es[k, m * 8 : m * 8 + 8, 127:128], (8, 128))
            corner = jnp.where(lane == 16 * m + 2 * row + 1, piece, corner)
        cys[k] = jnp.broadcast_to(jnp.sum(corner, axis=0, keepdims=True), (8, 128))
        pending[k] += [
            send(hs.at[k], hr.at[k], k * 6 + 1, dev(1, 0)),
            send(ys.at[k], yr_up.at[k], k * 6 + 2, dev(0, -1)),
            send(ys.at[k], yr_down.at[k], k * 6 + 3, dev(0, 1)),
            send(cxs.at[k], cxr.at[k], k * 6 + 4, dev(1, -1)),
            send(cys.at[k], cyr.at[k], k * 6 + 5, dev(-1, 1)),
        ]

    has_next_x = jnp.where(gx < n_gx - 1, 1.0, 0.0)
    has_previous_x = jnp.where(gx > 0, 1.0, 0.0)
    has_next_y = jnp.where(gy < n_gy - 1, 1.0, 0.0)
    has_previous_y = jnp.where(gy > 0, 1.0, 0.0)

    def add_rows(ref, c, value):
        ref[pl.ds(c * ROWS + 7, NZ, stride=8), :] = rows_at(ref, c, 7) + value

    def borders(s, k):
        ref = states[s]
        for copy in pending[k]:
            copy.wait_recv()
        add_rows(ref, 4, er[k, NZ : 2 * NZ, :] * (TIME_STEP * has_next_x))
        add_rows(ref, 5, er[k, 0:NZ, :] * (-TIME_STEP * has_next_x))
        hrow[k, 0:NZ, :] = (hr[k, 0:NZ, :] + TIME_STEP * es[k, NZ : 2 * NZ, :]) * has_previous_x
        for m in range(NZ // 8):
            o = m * 8
            side = jnp.where(lane == 127, pltpu.roll(cxr[k], 127 - m, 1), 0.0) * (TIME_STEP * has_next_y)
            hrow[k, NZ + o : NZ + o + 8, :] = (
                hr[k, NZ + o : NZ + o + 8, :] - TIME_STEP * es[k, o : o + 8, :] + side
            ) * has_previous_x
        corner = jnp.where(row == 7, cyr[k], 0.0) * (TIME_STEP * has_next_x)
        even = (lane & 1) == 0
        return [
            jnp.where(
                even,
                pltpu.roll(up_e, 127, 1) * (factor * has_next_y),
                (down_h + factor * own_e - other) * has_previous_y,
            )
            for up_e, down_h, own_e, factor, other in (
                (yr_up[k, 8:16, :], pltpu.roll(yr_down[k, 0:8, :], 1, 1), ys[k, 8:16, :], -TIME_STEP, zero),
                (yr_up[k, 0:8, :], pltpu.roll(yr_down[k, 8:16, :], 1, 1), ys[k, 0:8, :], TIME_STEP, corner),
            )
        ]

    def electric_block(s, k, sides, b):
        ref = states[s]
        moved = [pltpu.roll(side, 128 - b * (2 * ZB), 1) for side in sides]
        hx, hy, hz = ([at(ref, c, b, j) for j in range(-1 if c < 5 else 0, ZB)] for c in (3, 4, 5))
        hx[0] = jnp.where(b > 0, hx[0], 0.0)
        hy[0] = jnp.where(b > 0, hy[0], 0.0)
        old = [[at(ref, c, b, j) for c in range(3)] for j in range(ZB)]
        us = [at(scale, 0, b, j) for j in range(ZB)]
        behind_hx, behind_hz = [], []
        for j in range(ZB):
            for n, values, o, out in ((0, hx, j + 1, behind_hx), (1, hz, j, behind_hz)):
                side = pltpu.roll(moved[n], 127 - 2 * j, 1)
                values[o] = values[o] + jnp.where(lane == 127, side, 0.0)
                out.append(values[o] - jnp.where(lane == 0, side, pltpu.roll(values[o], 1, 1)))
        new = []
        for j in range(ZB):

            def along_x(value, n, j=j):
                side = wide(hrow[k, pl.ds(n * NZ + b * ZB + j, 1), :])
                return value - jnp.where(row == 0, side, pltpu.roll(value, 1, 0))

            new.append(
                (
                    old[j][0] + us[j] * (behind_hz[j] - (hy[j + 1] - hy[j])),
                    old[j][1] + us[j] * ((hx[j + 1] - hx[j]) - along_x(hz[j], 1)),
                    old[j][2] + us[j] * (along_x(hy[j + 1], 0) - behind_hx[j]),
                )
            )
        for j in range(ZB):
            for n in range(3):
                put(ref, n, b, j, new[j][n])
            put(ref, 3, b, j, hx[j + 1])
            put(ref, 5, b, j, hz[j])
        return old, new

    def electric_step(s, k):
        sides = borders(s, k)

        def body(b, carry):
            electric_block(s, k, sides, b)
            return carry

        lax.fori_loop(0, NB, body, 0)
        e_rows(states[s], k + 2)
        send_e(k + 2)

    (a1, b1), (a2, b2) = weights_at(1), weights_at(2)
    k11, k12, k22 = (OMEGA**2 * k for k in (a1 * a1 - b1 * b1, a1 * a2 - b1 * b2, a2 * a2 - b2 * b2))

    def last_forward():
        sides = borders(0, 2)

        def body(b, carry):
            old, new = electric_block(0, 2, sides, b)
            for j in range(ZB):
                for n in range(3):
                    put(mixed, n, b, j, k11 * old[j][n] + k12 * new[j][n])
                    put(mixed, 3 + n, b, j, k12 * old[j][n] + k22 * new[j][n])
            return carry

        lax.fori_loop(0, NB, body, 0)

    def last_adjoint():
        sides = borders(1, 3)

        def body(b, carry):
            old, new = electric_block(1, 3, sides, b)
            for j in range(ZB):
                terms = [old[j][n] * at(mixed, n, b, j) + new[j][n] * at(mixed, 3 + n, b, j) for n in range(3)]
                put(sens_ref, 0, b, j, terms[0] + terms[1] + terms[2])
            return carry

        lax.fori_loop(0, NB, body, 0)

    for s in range(2):
        magnetic_half(s, s)

    def scales(b, carry):
        rows = pl.ds(pl.multiple_of(b * 192, 192), 192)
        scale[rows, :] = 0.5 / eps_ref[rows, :]
        return carry

    lax.fori_loop(0, ROWS // 192, scales, 0)

    for copy in a_copies:
        copy.wait_recv()

    for k in range(len(ROWS_UP)):
        dup[k * 8 : k * 8 + 8, :] = unpacked(cor_r[0:8, :], cor_r[8:16, :], k)
    for k in range(len(ROWS_DOWN)):
        ddown[k * 8 : k * 8 + 8, :] = unpacked(cor_r[16:24, :], cor_r[24:32, :], k)

    far_row = gx * 8 + jnp.where(row < 4, row + 8, row - 8)
    far_lane = gy * 128 + jnp.where(lane < 64, lane + 128, lane - 128)
    row_in = (far_row >= 0) & (far_row < n_gx * 8)
    lane_in = (far_lane >= 0) & (far_lane < n_gy * 128)
    inside = [[None, lane_in], [row_in, row_in & lane_in]]
    where_up, where_down = (
        {key: 8 * k + 4 * n for k, keys in enumerate(table) for n, key in enumerate(keys)}
        for table in (ROWS_UP, ROWS_DOWN)
    )

    def border_rows(up, down, c, z):
        o = z - Z0

        def get(ref, start):
            at_z = start + (o if start % 8 + o < 8 else 0)
            return wide(ref[at_z : at_z + 1, :])

        up0, down0 = get(up, where_up[(c, 0)]), get(down, where_down[(c, 7)])
        out = jnp.where(row < 4, up0, down0)
        if (c, 1) in where_up:
            out = jnp.where(row == 1, get(up, where_up[(c, 1)]), out)
        if (c, 6) in where_down:
            out = jnp.where(row == 6, get(down, where_down[(c, 6)]), out)
        return out

    def masked(q, other=0.0):
        return [
            [q[r][n] if inside[r][n] is None else jnp.where(inside[r][n], q[r][n], other) for n in range(2)]
            for r in range(2)
        ]

    def extended(c, z):
        k = TILES_Y.index((c, z))
        q = [
            [tile(c, z), unpacked(col_r[0:8, :], col_r[8:16, :], k)],
            [border_rows(up_r, down_r, c, z), border_rows(dup, ddown, c, z)],
        ]
        return masked(q, 1.0 if c == 6 else 0.0)

    def combine(fn, *qs):
        return [[fn(*[q[r][n] for q in qs]) for n in range(2)] for r in range(2)]

    def turn_x(q, shift, edge):
        out = [[None, None], [None, None]]
        for n in range(2):
            first, second = pltpu.roll(q[0][n], shift, 0), pltpu.roll(q[1][n], shift, 0)
            out[0][n] = jnp.where(row == edge, second, first)
            out[1][n] = jnp.where(row == edge, first, second)
        return out

    def turn_y(q, shift, edge):
        out = []
        for r in range(2):
            first, second = pltpu.roll(q[r][0], shift, 1), pltpu.roll(q[r][1], shift, 1)
            out.append([jnp.where(lane == edge, second, first), jnp.where(lane == edge, first, second)])
        return out

    def ahead_x(q):
        return combine(jnp.subtract, turn_x(q, 7, 7), q)

    def ahead_y(q):
        return combine(jnp.subtract, turn_y(q, 127, 127), q)

    def behind_x(q):
        return combine(jnp.subtract, q, turn_x(q, 1, 0))

    def behind_y(q):
        return combine(jnp.subtract, q, turn_y(q, 1, 0))

    def half(h, one, two):
        return masked(combine(lambda h, p, q: h - TIME_STEP * (p - q), h, one, two))

    def full(e, us, one, two):
        return masked(combine(lambda e, us, p, q: e + us * (p - q), e, us, one, two))

    def minus(p, q):
        return combine(jnp.subtract, p, q)

    def magnetic(e, h, zs):
        for z in zs:
            ex, ey, ez = (e[(c, z)] for c in range(3))
            h[(3, z)] = half(h[(3, z)], ahead_y(ez), minus(e[(1, z + 1)], ey))
            h[(4, z)] = half(h[(4, z)], minus(e[(0, z + 1)], ex), ahead_x(ez))
            h[(5, z)] = half(h[(5, z)], ahead_x(ey), ahead_y(ex))

    e = {(c, z): extended(c, z) for c, z in TILES_Y if c < 3}
    h = {(c, z): extended(c, z) for c, z in TILES_Y if 3 <= c < 6}
    us = {z: combine(lambda p: 0.5 / p, extended(6, z)) for c, z in TILES_Y if c == 6}
    magnetic(e, h, range(Z0, Z0 + 4))
    h1 = [h[(3, ZM)][0][0], h[(4, ZM)][0][0]]
    for z in range(Z0 + 1, Z0 + 4):
        hx, hy, hz = (h[(c, z)] for c in (3, 4, 5))
        e[(0, z)] = full(e[(0, z)], us[z], behind_y(hz), minus(hy, h[(4, z - 1)]))
        e[(1, z)] = full(e[(1, z)], us[z], minus(hx, h[(3, z - 1)]), behind_x(hz))
        e[(2, z)] = full(e[(2, z)], us[z], behind_x(hy), behind_y(hx))
    e1 = [e[(0, ZM)][0][0], e[(1, ZM)][0][0]]
    magnetic(e, h, range(Z0 + 1, Z0 + 3))
    h2 = [h[(3, ZM)][0][0], h[(4, ZM)][0][0]]
    hz = h[(5, ZM)]
    us_m = us[ZM][0][0]
    e2 = [
        e1[0] + us_m * (behind_y(hz)[0][0] - (h2[1] - h[(4, ZM - 1)][0][0])),
        e1[1] + us_m * ((h2[0] - h[(3, ZM - 1)][0][0]) - behind_x(hz)[0][0]),
    ]
    for part_of in range(2):
        first, second = weights_at(0.5)[part_of], weights_at(1.5)[part_of]
        hx, hy = (first * h1[n] + second * h2[n] for n in range(2))
        first, second = weights_at(1)[part_of], weights_at(2)[part_of]
        ex, ey = (first * e1[n] + second * e2[n] for n in range(2))
        for n, value in enumerate((-hy, hx, ey, -ex)):
            gath[0, (part_of * 4 + n) * 8 : (part_of * 4 + n) * 8 + 8, :] = value

    base_g = base + 8
    g_copies = [send(gath.at[0], gath.at[d], base_g + d - 1, zh_peer(d)) for d in range(1, n_zh)]

    for copy in load_rest:
        copy.wait()
    n_w = n_xi * 2 * n_gy
    n_k = n_zh * 16
    wrow = iota((n_w, 128), 0)
    wlane = iota((n_w, 128), 1)
    u = zh * (n_xi * n_gy) + (wrow // (2 * n_gy)) * n_gy + wrow % n_gy
    imag_out = (wrow // n_gy) % 2
    back = wlane // 16
    imag_in = (wlane // 8) % 2
    x = (((zh - back + n_zh) % n_zh) * n_xi + xi) * 8 + wlane % 8
    n_u = n_gx * n_gy
    weights = cos_turns((2 * u + 1 - n_u) * x * (4096 // (16 * n_u)) + 1024 * (imag_out - imag_in))
    hits = jnp.zeros((n_w, 128), F32)
    for d in range(n_zh):
        t = tile_of(d)
        same = (lists_ref[d, pl.ds(t % 8, 1), :] == u[:, : lists_ref.shape[2]]).astype(F32)
        count = jnp.sum(same, axis=1, keepdims=True) * mask_ref[t].astype(F32)
        hits = jnp.where(back == d, count, hits)
    wtab[0], wtab[1] = halves(weights * hits)

    def v_rows(b, carry):
        y = b * 32 + iota((32, 512), 0)
        v = iota((32, 512), 1)
        rows = pl.ds(pl.multiple_of(b * 32, 32), 32)
        vtab[0, rows, :], vtab[1, rows, :] = halves(cos_turns((2 * (v & 255) - 255) * y - 1024 * (v >> 8)))
        return carry

    lax.fori_loop(0, 4, v_rows, 0)
    d = iota((n_gy, 512), 0)
    v = iota((n_gy, 512), 1)
    tws[...] = cos_turns((2 * (v & 255) - 255) * (((gy - d + n_gy) % n_gy) * 128) - 1024 * (v >> 8))

    electric_step(0, 0)
    magnetic_half(0, 2)

    for copy in g_copies:
        copy.wait_recv()
    table = (wtab[0][:, 0:n_k], wtab[1][:, 0:n_k])
    blk = 8 * n_gy
    for c in range(4):
        planes = jnp.concatenate(
            [gath[d, (4 * r + c) * 8 : (4 * r + c) * 8 + 8, :] for d in range(n_zh) for r in range(2)], axis=0
        )
        out = product(table, halves(planes))
        for q in range(n_xi):
            for r in range(2):
                part[q * blk + r * 4 * n_gy + c * n_gy : q * blk + r * 4 * n_gy + (c + 1) * n_gy, :] = out[
                    (q * 2 + r) * n_gy : (q * 2 + r + 1) * n_gy, :
                ]
    base_r = base_g + n_zh - 1
    r_copies = []
    for d in range(1, n_xi):
        to = (xi + d) % n_xi
        r_copies.append(
            send(
                part.at[pl.ds(pl.multiple_of(to * blk, blk), blk)], part_r.at[d - 1], base_r + d - 1, xi_peer(d)
            )
        )

    electric_step(1, 1)
    magnetic_half(1, 3)

    for copy in r_copies:
        copy.wait_recv()
    acc = part[pl.ds(pl.multiple_of(xi * blk, blk), blk), :]
    for d in range(1, n_xi):
        acc = acc + part_r[d - 1]
    total[...] = acc
    for j in range(n_gy):
        rows_s[j] = total[pl.ds(j, 8, stride=n_gy), :]
    rows_r[0] = rows_s[gy]
    base_a = base_r + n_xi - 1
    last_copies = []
    for d in range(1, n_gy):
        to = (gy + d) % n_gy
        last_copies.append(
            send(rows_s.at[to], rows_r.at[d], base_a + d - 1, {"gx": gx, "gy": to})
        )

    last_forward()
    last_adjoint()

    for copy in started:
        copy.wait_send()
    for copy in last_copies:
        copy.wait_recv()
    turned = product(halves(rows_r[...].reshape(n_gy * 8, 128)), (vtab[0], vtab[1]))
    sign = jnp.where(iota((8, 256), 0) < 4, 1.0, -1.0)
    out = jnp.zeros((8, 256), F32)
    for d in range(n_gy):
        rows = turned[d * 8 : d * 8 + 8, :]
        value = rows[:, :256] + sign * pltpu.roll(rows[:, 256:], 4, 0)
        out = out + tws[d : d + 1, :256] * value + tws[d : d + 1, 256:] * (sign * pltpu.roll(value, 4, 0))
    far_ref[...] = out * (1.0 / math.sqrt(CX * CY))


PIECES = ((0, 4), (1, 4), (2, 1), (3, 1))


def write_out(*refs):
    sems = refs[-1]
    copies = []
    for i, pieces in PIECES:
        rows = refs[i].shape[0] // pieces
        for p in range(pieces):
            part = pl.ds(p * rows, rows)
            copies.append(pltpu.make_async_copy(refs[i].at[part], refs[4 + i].at[part], sems.at[len(copies)]))
    for copy in copies:
        copy.start()
    for copy in copies:
        copy.wait()


def solution(mesh):
    n_gx, n_gy = mesh.shape["gx"], mesh.shape["gy"]
    n_xi = 4 if n_gx == 16 else n_gx
    dims = (n_gx // n_xi, n_xi, n_gy)
    n_zh = dims[0]
    n_sem = 24 + 8 + (n_zh - 1) + (n_xi - 1) + (n_gy - 1)
    vmem = pl.BlockSpec(memory_space=pltpu.VMEM)
    hbm = pl.BlockSpec(memory_space=pltpu.HBM)
    blk = 8 * n_gy

    def buffer(*shape):
        return pltpu.VMEM(shape, F32)

    def shards(fields, adjoint, permittivity, lists, mask):
        shapes = (
            jax.ShapeDtypeStruct((6 * ROWS, 128), F32),
            jax.ShapeDtypeStruct((6 * ROWS, 128), F32),
            jax.ShapeDtypeStruct((ROWS, 128), F32),
            jax.ShapeDtypeStruct((8, 256), F32),
        )
        made = pl.pallas_call(
            functools.partial(kernel, dims),
            out_shape=tuple(pltpu.VMEM(shape.shape, F32) for shape in shapes),
            in_specs=[hbm] * 5,
            out_specs=(vmem,) * 4,
            scratch_shapes=[
                buffer(ROWS, 128),
                pltpu.VMEM((n_zh, 8, lists.shape[1]), jnp.int32),
                pltpu.SMEM(mask.shape, jnp.int32),
                buffer(ROWS, 128),
                buffer(6 * 64, 128), buffer(6 * ROWS, 128),
                buffer(4, 2 * NZ, 128), buffer(4, 2 * NZ, 128), buffer(4, 2 * NZ, 128), buffer(4, 2 * NZ, 128),
                buffer(4, 16, 128), buffer(4, 16, 128), buffer(4, 16, 128),
                buffer(4, 8, 128), buffer(4, 8, 128), buffer(4, 8, 128), buffer(4, 8, 128),
                buffer(4, 2 * NZ, 128),
                buffer(8 * N_UP, 128), buffer(8 * N_DOWN, 128), buffer(16, 128), buffer(32, 128),
                buffer(8 * N_UP, 128), buffer(8 * N_DOWN, 128), buffer(16, 128), buffer(32, 128),
                buffer(8 * N_UP, 128), buffer(8 * N_DOWN, 128),
                buffer(n_zh, 64, 128), pltpu.VMEM((2, n_xi * 2 * n_gy, 128), jnp.bfloat16), pltpu.VMEM((2, 128, 512), jnp.bfloat16), buffer(n_gy, 512),
                buffer(n_xi * blk, 128), buffer(max(n_xi - 1, 1), blk, 128), buffer(blk, 128),
                buffer(n_gy, 8, 128), buffer(n_gy, 8, 128),
                pltpu.SemaphoreType.DMA((4 + n_zh + 6,)),
                pltpu.SemaphoreType.DMA((n_sem,)),
                pltpu.SemaphoreType.DMA((n_sem,)),
            ],
            compiler_params=pltpu.CompilerParams(
                collective_id=0, has_side_effects=True, vmem_limit_bytes=40 * 1024 * 1024
            ),
        )(
            *[
                pltpu.with_memory_space_constraint(value, pltpu.HBM)
                for value in (
                    fields.reshape(6 * ROWS, 128),
                    adjoint.reshape(6 * ROWS, 128),
                    permittivity.reshape(ROWS, 128),
                    lists,
                    mask,
                )
            ]
        )
        out = pl.pallas_call(
            write_out,
            out_shape=shapes,
            in_specs=[pl.BlockSpec(memory_space=pl.ANY)] * 4,
            out_specs=(pl.BlockSpec(memory_space=pl.ANY),) * 4,
            scratch_shapes=[pltpu.SemaphoreType.DMA((10,))],
            compiler_params=pltpu.CompilerParams(vmem_limit_bytes=1024 * 1024),
        )(*made)
        return (
            out[0].reshape(fields.shape),
            out[1].reshape(fields.shape),
            out[2].reshape(permittivity.shape),
            out[3].reshape(1, 8, 256),
        )

    in_specs = (P(None, None, "gx", "gy"), P(None, None, "gx", "gy"), P(None, "gx", "gy"), P(), P())
    out_specs = (
        P(None, None, "gx", "gy"),
        P(None, None, "gx", "gy"),
        P(None, "gx", "gy"),
        P(("gx", "gy"), None, None),
    )
    return jax.shard_map(shards, mesh=mesh, in_specs=in_specs, out_specs=out_specs, check_vma=False)
```
